768 devices in a mesh: dp: 96 (over z, y), sub: 8 (over x, core).
Axes of the slice: x: 4, y: 8, z: 12, core: 2. Of those that a mesh axis runs over, the one named last changes fastest.
Arguments:
- embeddings: bfloat16 [393216, 1024], P(('dp', 'sub')), may hold values from -6 to 6
- rotation: bfloat16 [1024, 1024], replicated, may hold values from -0.1875 to 0.1875
- centroids: bfloat16 [96, 1024], replicated, may hold values from -6 to 6
- assignments: int32 [393216], P(('dp', 'sub')), may hold values from 0 to 95
- codes: int32 [393216, 64], P(('dp', 'sub')), may hold values from 0 to 255
Outputs:
- gram: float32 [1024, 1024], P('sub')
- coarse_sums: float32 [96, 1024], P('dp', 'sub')
- codebook_sums: float32 [256, 1024], P(None, 'sub')
The draws below stay inside these ranges and needn't reach their ends.
All inputs are finite; a program needn't handle non-finite values.
Results may differ from the reference program's by a relative error of at most 0.0045.
Values may be sent and summed in bfloat16 or wider, within the bound.
No kernel may reach another device: no remote copies, remote signals or barrier semaphores. Data moves between devices by JAX's collectives and lax.ppermute only.
A program may use at most 32 MiB of HBM per device.

```python
import math
import jax
import jax.numpy as jnp
import numpy as np
from jax import lax

D = 1024
M = 64
K = 256
VEC_DEV = 512
VECS = 393216
CENTS = 96
N_SUB = 8


def place_ends(values, key, smallest, top_value):
    longest = values.shape.index(max(values.shape))
    spots = []
    for shift in (0, 1):
        where = [jax.random.randint(jax.random.fold_in(key, axis), (), 0, length) for axis, length in enumerate(values.shape)]
        where[longest] = (where[longest] + shift) % values.shape[longest]
        spots.append(tuple(where))
    return values.at[spots[0]].set(smallest).at[spots[1]].set(top_value)


def block_levels(rng, extent, cuts, smallest, largest):
    def one(dim, shards_of):
        draws = jax.random.uniform(jax.random.fold_in(jax.random.fold_in(rng, 6), dim), (shards_of,), jnp.float32, smallest / len(cuts), largest / len(cuts))
        return jnp.repeat(jnp.exp(draws), extent[dim] // shards_of).reshape((-1,) + (1,) * (len(extent) - dim - 1))

    factor_of = one(*cuts[0])
    for cut in cuts[1:]:
        factor_of = factor_of * one(*cut)
    return factor_of


def rank_bounds(amount, lean):
    weights = [(1 << 20) // math.isqrt(standing ** lean) + 1 for standing in range(1, amount + 1)]
    scale = 1 + sum(weights) // (1 << 30)
    return np.cumsum(np.array([max(1, weight // scale) for weight in weights]))


def ranked_ids(stream_key, dims, number_of, skew):
    grid = rank_bounds(number_of, skew)
    ticket = jax.random.randint(jax.random.fold_in(stream_key, 1), dims, 0, int(grid[number_of - 1]))
    standing = jnp.searchsorted(jnp.asarray(grid, jnp.int32), ticket, side="right")
    return jax.random.permutation(jax.random.fold_in(stream_key, 2), number_of)[standing].astype(jnp.int32)


def bell_draw(key, extent, scale, most, split=(), held_as=jnp.bfloat16):
    factor_of = block_levels(key, extent, split, -0.22, 0.18) if split else 1.0
    entries = jax.random.normal(key, extent, jnp.float32) * scale * factor_of
    return jnp.minimum(jnp.maximum(entries, -most), most).astype(held_as)


def setup_inputs(seed: int = 0) -> dict:
    arg_keys = jax.random.split(jax.random.key(seed), 6)
    return {
        "embeddings": bell_draw(arg_keys[0], (VECS, D), 1.0, 6.0, ((0, 768),)),
        "rotation": bell_draw(arg_keys[1], (D, D), D ** -0.5, 0.1875),
        "centroids": bell_draw(arg_keys[2], (CENTS, D), 1.0, 6.0),
        "assignments": place_ends(ranked_ids(arg_keys[3], (VECS,), CENTS, 1), jax.random.fold_in(arg_keys[3], 3), 0, CENTS - 1).astype(jnp.int32),
        "codes": place_ends(jax.random.randint(arg_keys[4], (VECS, M), 0, K), jax.random.fold_in(arg_keys[4], 1), 0, K - 1).astype(jnp.int32),
    }


def reference(embeddings, rotation, centroids, assignments, codes):
    block = VEC_DEV * N_SUB
    count = VECS // block
    subw = D // M
    emb_blocks = embeddings.reshape(count, block, D)
    asg_blocks = assignments.reshape(count, block)
    code_blocks = codes.reshape(count, block, M)
    offsets = (jnp.arange(M, dtype=jnp.int32) * K)[None, :]

    def advance(carry, item):
        gram, coarse, book = carry
        rows, asg, code = item
        groups = rows.reshape(N_SUB, VEC_DEV, D).astype(jnp.float32)
        parts = jnp.einsum("gvi,gvj->gij", groups, groups).astype(jnp.bfloat16)
        gram = gram + jnp.sum(parts.astype(jnp.float32), axis=0)
        rotated = jnp.dot(rows, rotation, preferred_element_type=jnp.float32)
        residual = (rotated - centroids[asg].astype(jnp.float32)).astype(jnp.bfloat16)
        wide = residual.astype(jnp.float32)
        coarse = coarse + jax.ops.segment_sum(wide, asg, num_segments=CENTS)
        pieces = wide.reshape(block * M, subw)
        labels = (code + offsets).reshape(block * M).astype(jnp.int32)
        book = book + jax.ops.segment_sum(pieces, labels, num_segments=M * K)
        return (gram, coarse, book), None

    start = (jnp.zeros((D, D), jnp.float32), jnp.zeros((CENTS, D), jnp.float32),
             jnp.zeros((M * K, subw), jnp.float32))
    (gram, coarse, book), _ = lax.scan(advance, start, (emb_blocks, asg_blocks, code_blocks))
    gram = gram / VECS
    coarse = coarse * (CENTS / VECS) ** 0.5
    book = book.reshape(M, K, subw).transpose(1, 0, 2).reshape(K, D) * (K / VECS) ** 0.5
    return gram, coarse, book
```

```python
import jax
import jax.numpy as jnp
from jax import lax
from jax.experimental import pallas as pl
from jax.experimental.pallas import tpu as pltpu
from jax.sharding import Mesh
from jax.sharding import PartitionSpec as P

D = 1024
M = 64
K = 256
CENTS = 96
LANES = 128
X = 4
DP = ("z", "y")
DP_SUB = ("z", "y", "x", "c")
BOOK0 = D
COARSE0 = D + K
ROWS = D + K + CENTS
PIECE = 14
CHUNK = 16
bf16 = jnp.bfloat16
f16 = jnp.float16
f32 = jnp.float32
VMEM = pl.BlockSpec(memory_space=pltpu.VMEM)
SMEM = pl.BlockSpec(memory_space=pltpu.SMEM)


def dot(a, b):
    return jnp.dot(a, b, preferred_element_type=f32)


def partial_sums(core_ref, e0, e1, rot, cent, p0, p1, out, turned, res):
    core = core_ref[0]
    rows = e0.shape[0]
    halves = ((e0, p0), (e1, p1))

    def columns(x):
        return pl.ds(pl.multiple_of((2 * x + core) * LANES, LANES), LANES)

    for x in range(X):
        for h, (e, _) in enumerate(halves):
            turned[x * LANES : (x + 1) * LANES, h * rows : (h + 1) * rows] = e[:, columns(x)].T
    wide = 256
    for n in range(D // wide):
        cols = slice(n * wide, (n + 1) * wide)
        g = dot(turned[:, :rows], e0[:, cols]) + dot(turned[:, rows:], e1[:, cols])
        for x in range(X):
            for k in range(wide // LANES):
                j = n * (wide // LANES) + k
                out[x, j * LANES : (j + 1) * LANES, :] = g[
                    x * LANES : (x + 1) * LANES, k * LANES : (k + 1) * LANES
                ].astype(bf16)

    label = lax.broadcasted_iota(jnp.int32, (CENTS, rows), 0)
    picks = [(label == p[M : M + 1, :]).astype(bf16) for _, p in halves]
    for q in range(X // 2):
        r = jnp.concatenate([rot[:, columns(2 * q)], rot[:, columns(2 * q + 1)]], axis=1)
        c = jnp.concatenate([cent[:, columns(2 * q)], cent[:, columns(2 * q + 1)]], axis=1)
        coarse = jnp.zeros((CENTS, 2 * LANES), f32)
        for h, (e, _) in enumerate(halves):
            base = lax.dot_general(picks[h], c, (((0,), (0,)), ((), ())), preferred_element_type=f32)
            residual = (dot(e[...], r) - base).astype(bf16)
            res[h * rows : (h + 1) * rows, q * 2 * LANES : (q + 1) * 2 * LANES] = residual
            coarse += dot(picks[h], residual)
        for k in range(2):
            out[2 * q + k, COARSE0:ROWS, :] = coarse[:, k * LANES : (k + 1) * LANES].astype(bf16)

    word = lax.broadcasted_iota(jnp.int32, (K, rows), 0)
    lane = lax.broadcasted_iota(jnp.int32, (rows, LANES), 1)
    subs = M // 8

    def book(x, carry):
        total = jnp.zeros((K, LANES), f32)
        for h, (_, p) in enumerate(halves):
            first = pl.multiple_of((2 * x + core) * subs, subs)
            codes = p[pl.ds(first, subs), :]
            mine = res[h * rows : (h + 1) * rows, pl.ds(pl.multiple_of(x * LANES, LANES), LANES)]
            for m in range(subs):
                onehot = (word == codes[m : m + 1, :]).astype(bf16)
                part = jnp.where(lane // (LANES // subs) == m, mine, jnp.zeros_like(mine))
                total += dot(onehot, part)
        out[x, BOOK0:COARSE0, :] = total.astype(bf16)
        return carry

    lax.fori_loop(0, X, book, 0)


def first_sums(arrived, out, total):
    total[: ROWS, :] = arrived[...].astype(f32).sum(axis=0)
    peers = out.shape[0]
    zeros = jnp.zeros((CHUNK - PIECE - 1, LANES), f32)
    for i in range(peers):
        size = min(PIECE, max(0, COARSE0 - i * PIECE))
        parts = []
        if size:
            parts.append(total[i * PIECE : i * PIECE + size, :])
        if size < PIECE:
            parts.append(jnp.zeros((PIECE - size, LANES), f32))
        parts += [total[COARSE0 + i : COARSE0 + i + 1, :], zeros]
        out[i] = jnp.concatenate(parts, axis=0).astype(bf16)


def owned_sums(place_ref, arrived, coarse, mine, *, vectors):
    total = arrived[...].astype(f32).sum(axis=0)
    row = lax.broadcasted_iota(jnp.int32, (CHUNK, LANES), 0)
    coarse[...] = total[PIECE : PIECE + 1, :] * (CENTS / vectors) ** 0.5
    in_gram = place_ref[0] * PIECE + row < D
    total = total * jnp.where(in_gram, 1.0 / vectors, (K / vectors) ** 0.5)
    total = jnp.where(row < PIECE, total, 0.0)
    top = jnp.max(jnp.abs(total), keepdims=True)
    power = jnp.ceil(jnp.log2(jnp.maximum(top, 2.0**-100)))
    total = total * jnp.exp2(-power)
    total = jnp.where(row < PIECE, total, jnp.broadcast_to(power, total.shape))
    mine[...] = total


def laid_out(arrived, gram, book, flat):
    for i in range(arrived.shape[0]):
        size = min(PIECE, max(0, COARSE0 - i * PIECE))
        if size:
            piece = arrived[i]
            power = jnp.exp2(piece[PIECE : PIECE + 1, :])
            flat[i * PIECE : i * PIECE + size, :] = piece[:size] * power
    for j in range(D // LANES):
        gram[:, j * LANES : (j + 1) * LANES] = flat[j * LANES : (j + 1) * LANES, :]
    book[...] = flat[BOOK0:COARSE0, :]


def per_device(embeddings, rotation, centroids, assignments, codes):
    rows = embeddings.shape[0]
    peers = lax.axis_size(DP)
    vectors = rows * peers * lax.axis_size(("x", "c"))
    core = lax.axis_index("c").reshape(1)
    place = lax.axis_index(DP).reshape(1)
    words = jnp.concatenate([codes.T, jnp.broadcast_to(assignments[None, :], (8, rows))], axis=0)
    swap = [(0, 1), (1, 0)]
    other = lax.ppermute(embeddings, "c", swap)
    other_words = lax.ppermute(words, "c", swap)
    parts = pl.pallas_call(
        partial_sums,
        out_shape=jax.ShapeDtypeStruct((X, ROWS, LANES), bf16),
        in_specs=[SMEM] + [VMEM] * 6,
        out_specs=VMEM,
        scratch_shapes=[pltpu.VMEM((D // 2, 2 * rows), bf16), pltpu.VMEM((2 * rows, D // 2), bf16)],
        compiler_params=pltpu.CompilerParams(vmem_limit_bytes=48 * 2**20),
        name="partial_sums",
    )(core, embeddings, other, rotation, centroids, words, other_words)
    arrived = lax.all_to_all(parts, "x", split_axis=0, concat_axis=0, tiled=True)
    pieces = pl.pallas_call(
        first_sums,
        out_shape=jax.ShapeDtypeStruct((peers, CHUNK, LANES), bf16),
        in_specs=[VMEM],
        out_specs=VMEM,
        scratch_shapes=[pltpu.VMEM((ROWS, LANES), f32)],
        name="first_sums",
    )(arrived)
    arrived = lax.all_to_all(pieces, DP, split_axis=0, concat_axis=0, tiled=True)
    coarse_sums, mine = pl.pallas_call(
        lambda *refs: owned_sums(*refs, vectors=vectors),
        out_shape=(
            jax.ShapeDtypeStruct((1, LANES), f32),
            jax.ShapeDtypeStruct((CHUNK, LANES), f32),
        ),
        in_specs=[SMEM, VMEM],
        out_specs=(VMEM, VMEM),
        name="owned_sums",
    )(place, arrived)
    spread = jnp.broadcast_to(mine.astype(f16)[None], (peers, CHUNK, LANES))
    arrived = lax.all_to_all(spread, DP, split_axis=0, concat_axis=0, tiled=True)
    gram, codebook_sums = pl.pallas_call(
        laid_out,
        out_shape=(jax.ShapeDtypeStruct((LANES, D), f32), jax.ShapeDtypeStruct((K, LANES), f32)),
        in_specs=[VMEM],
        out_specs=(VMEM, VMEM),
        scratch_shapes=[pltpu.VMEM((COARSE0, LANES), f32)],
        name="laid_out",
    )(arrived.astype(f32))
    return gram, coarse_sums, codebook_sums


def solution(mesh):
    finer = Mesh(mesh.devices.reshape(12, 8, X, 2), DP_SUB)
    return jax.shard_map(
        per_device,
        mesh=finer,
        in_specs=(P(DP_SUB, None), P(), P(), P(DP_SUB), P(DP_SUB, None)),
        out_specs=(P(("x", "c"), None), P(DP, ("x", "c")), P(None, ("x", "c"))),
        check_vma=False,
    )
```

```python
import jax
import jax.numpy as jnp
from jax import lax
from jax.experimental import pallas as pl
from jax.experimental.pallas import tpu as pltpu
from jax.sharding import Mesh
from jax.sharding import PartitionSpec as P

D = 1024
M = 64
K = 256
CENTS = 96
LANES = 128
X = 4
Y = 8
ZF = 2
ZS = 6
OWNERS = ("zf", "y")
PEERS = ZF * Y
DP = ("zs", "zf", "y")
DP_SUB = ("zs", "zf", "y", "x", "c")
BOOK0 = D
COARSE0 = D + K
ROWS = D + K + CENTS
GP = D // PEERS
BP = K // PEERS
CP = CENTS // PEERS
C0 = GP + BP
PART = C0 + 16
ONE = PART + BP
SPREAD = C0 + 8
bf16 = jnp.bfloat16
f16 = jnp.float16
f32 = jnp.float32
VMEM = pl.BlockSpec(memory_space=pltpu.VMEM)
SMEM = pl.BlockSpec(memory_space=pltpu.SMEM)


def params(mib):
    return pltpu.CompilerParams(vmem_limit_bytes=mib * 2**20)


def dot(a, b):
    return jnp.dot(a, b, preferred_element_type=f32)


def partial_sums(core_ref, place_ref, e0, e1, rot, cent, p0, p1, out, turned, res):
    core = core_ref[0]
    rows = e0.shape[0]
    halves = ((e0, p0), (e1, p1))

    def columns(x):
        return pl.ds(pl.multiple_of((2 * x + core) * LANES, LANES), LANES)

    for x in range(X):
        for h, (e, _) in enumerate(halves):
            turned[x * LANES : (x + 1) * LANES, h * rows : (h + 1) * rows] = e[:, columns(x)].T
    wide = 256
    for n in range(D // wide):
        cols = slice(n * wide, (n + 1) * wide)
        g = dot(turned[:, :rows], e0[:, cols]) + dot(turned[:, rows:], e1[:, cols])
        for x in range(X):
            for k in range(wide // LANES):
                j = n * (wide // LANES) + k
                out[x, j * LANES : (j + 1) * LANES, :] = g[
                    x * LANES : (x + 1) * LANES, k * LANES : (k + 1) * LANES
                ].astype(bf16)

    label = lax.broadcasted_iota(jnp.int32, (CENTS, rows), 0)
    per_zf = CENTS // ZF
    sent = ((label % CP) * ZF + label // per_zf) * Y + (label // CP) % Y
    picks = [(label == p[M : M + 1, :]).astype(bf16) for _, p in halves]
    sends = [(sent == p[M : M + 1, :]).astype(bf16) for _, p in halves]
    for q in range(X // 2):
        r = jnp.concatenate([rot[:, columns(2 * q)], rot[:, columns(2 * q + 1)]], axis=1)
        c = jnp.concatenate([cent[:, columns(2 * q)], cent[:, columns(2 * q + 1)]], axis=1)
        coarse = jnp.zeros((CENTS, 2 * LANES), f32)
        for h, (e, _) in enumerate(halves):
            base = lax.dot_general(picks[h], c, (((0,), (0,)), ((), ())), preferred_element_type=f32)
            residual = (dot(e[...], r) - base).astype(bf16)
            res[h * rows : (h + 1) * rows, q * 2 * LANES : (q + 1) * 2 * LANES] = residual
            coarse += dot(sends[h], residual)
        for k in range(2):
            out[2 * q + k, COARSE0:ROWS, :] = coarse[:, k * LANES : (k + 1) * LANES].astype(bf16)

    word = lax.broadcasted_iota(jnp.int32, (K, rows), 0)
    lane = lax.broadcasted_iota(jnp.int32, (rows, LANES), 1)
    subs = M // 8

    def book(x, carry):
        total = jnp.zeros((K, LANES), f32)
        for h, (_, p) in enumerate(halves):
            first = pl.multiple_of((2 * x + core) * subs, subs)
            codes = p[pl.ds(first, subs), :]
            mine = res[h * rows : (h + 1) * rows, pl.ds(pl.multiple_of(x * LANES, LANES), LANES)]
            for m in range(subs):
                onehot = (word == codes[m : m + 1, :]).astype(bf16)
                part = jnp.where(lane // (LANES // subs) == m, mine, jnp.zeros_like(mine))
                total += dot(onehot, part)
        out[x, BOOK0:COARSE0, :] = total.astype(bf16)
        return carry

    lax.fori_loop(0, X, book, 0)


def first_sums(arrived, out):
    def summed(a, b):
        return arrived[:, a:b, :].astype(f32).sum(axis=0)

    coarse = summed(COARSE0, ROWS)
    zeros = jnp.zeros((PART - C0 - CP, LANES), f32)
    for q in range(PEERS):
        out[q, :GP, :] = summed(q * GP, (q + 1) * GP).astype(bf16)
        out[q, GP:C0, :] = summed(BOOK0 + q * BP, BOOK0 + (q + 1) * BP).astype(bf16)
        mine = coarse[q * CP : (q + 1) * CP, :]
        out[q, C0:PART, :] = jnp.concatenate([mine, zeros], axis=0).astype(bf16)


def second_sums(arrived, out):
    total = arrived[...].astype(f32).sum(axis=0)
    high = total.astype(bf16)
    low = total - high.astype(f32)
    coarse = jnp.concatenate([total[C0 : C0 + 8], low[C0 : C0 + 8]], axis=0).astype(bf16)
    book = low[GP:C0].astype(bf16)
    for i in range(out.shape[0]):
        out[i, :C0, :] = high[:C0]
        out[i, C0:PART, :] = coarse
        out[i, PART:ONE, :] = book


def owned_sums(place_ref, arrived, coarse_out, mine, *, vectors):
    total = arrived[...].astype(f32).sum(axis=0)
    coarse = total[C0 : C0 + 8] + total[C0 + 8 : C0 + 16]
    row = lax.broadcasted_iota(jnp.int32, (8, LANES), 0)
    own = jnp.where(row == place_ref[0], coarse, 0.0).sum(axis=0, keepdims=True)
    coarse_out[...] = own * (CENTS / vectors) ** 0.5
    gram = total[:GP] * (1.0 / vectors)
    book = (total[GP:C0] + total[PART:ONE]) * (K / vectors) ** 0.5

    def scaled(v):
        top = jnp.max(jnp.abs(v), keepdims=True)
        power = jnp.ceil(jnp.log2(jnp.maximum(top, 2.0**-100)))
        return v * jnp.exp2(-power), jnp.broadcast_to(power, (8, LANES))

    gram, gram_power = scaled(gram)
    book, book_power = scaled(book)
    mine[:GP, :] = gram
    mine[GP:C0, :] = book
    mine[C0:SPREAD, :] = jnp.where(row == 0, gram_power, book_power)


def laid_out(arrived, gram, book):
    for q in range(PEERS):
        power = jnp.exp2(arrived[q, C0:SPREAD, :])
        j, top = q * GP // LANES, q * GP % LANES
        gram[top : top + GP, j * LANES : (j + 1) * LANES] = arrived[q, :GP, :] * power[0:1]
        book[q * BP : (q + 1) * BP, :] = arrived[q, GP:C0, :] * power[1:2]


def per_device(embeddings, rotation, centroids, assignments, codes):
    rows = embeddings.shape[0]
    vectors = rows * lax.axis_size(DP_SUB)
    core = lax.axis_index("c").reshape(1)
    place = lax.axis_index("zs").reshape(1)
    words = jnp.concatenate([codes.T, jnp.broadcast_to(assignments[None, :], (8, rows))], axis=0)
    swap = [(0, 1), (1, 0)]
    other = lax.ppermute(embeddings, "c", swap)
    other_words = lax.ppermute(words, "c", swap)
    parts = pl.pallas_call(
        partial_sums,
        out_shape=jax.ShapeDtypeStruct((X, ROWS, LANES), bf16),
        in_specs=[SMEM] * 2 + [VMEM] * 6,
        out_specs=VMEM,
        scratch_shapes=[pltpu.VMEM((D // 2, 2 * rows), bf16), pltpu.VMEM((2 * rows, D // 2), bf16)],
        compiler_params=params(32),
        name="partial_sums",
    )(core, place, embeddings, other, rotation, centroids, words, other_words)
    arrived = lax.all_to_all(parts, "x", split_axis=0, concat_axis=0, tiled=True)
    pieces = pl.pallas_call(
        first_sums,
        out_shape=jax.ShapeDtypeStruct((PEERS, PART, LANES), bf16),
        in_specs=[VMEM],
        out_specs=VMEM,
        compiler_params=params(16),
        name="first_sums",
    )(arrived)
    arrived = lax.all_to_all(pieces, OWNERS, split_axis=0, concat_axis=0, tiled=True)
    pieces = pl.pallas_call(
        second_sums,
        out_shape=jax.ShapeDtypeStruct((ZS, ONE, LANES), bf16),
        in_specs=[VMEM],
        out_specs=VMEM,
        compiler_params=params(16),
        name="second_sums",
    )(arrived)
    arrived = lax.all_to_all(pieces, "zs", split_axis=0, concat_axis=0, tiled=True)
    coarse_sums, mine = pl.pallas_call(
        lambda *refs: owned_sums(*refs, vectors=vectors),
        out_shape=(
            jax.ShapeDtypeStruct((1, LANES), f32),
            jax.ShapeDtypeStruct((SPREAD, LANES), f32),
        ),
        in_specs=[SMEM, VMEM],
        out_specs=(VMEM, VMEM),
        compiler_params=params(16),
        name="owned_sums",
    )(place, arrived)
    spread = jnp.broadcast_to(mine.astype(f16)[None], (PEERS, SPREAD, LANES))
    arrived = lax.all_to_all(spread, OWNERS, split_axis=0, concat_axis=0, tiled=True)
    gram, codebook_sums = pl.pallas_call(
        laid_out,
        out_shape=(jax.ShapeDtypeStruct((LANES, D), f32), jax.ShapeDtypeStruct((K, LANES), f32)),
        in_specs=[VMEM],
        out_specs=(VMEM, VMEM),
        compiler_params=params(16),
        name="laid_out",
    )(arrived.astype(f32))
    return gram, coarse_sums, codebook_sums


def solution(mesh):
    finer = Mesh(mesh.devices.reshape(ZS, ZF, Y, X, 2), DP_SUB)
    return jax.shard_map(
        per_device,
        mesh=finer,
        in_specs=(P(DP_SUB, None), P(), P(), P(DP_SUB), P(DP_SUB, None)),
        out_specs=(P(("x", "c"), None), P(DP, ("x", "c")), P(None, ("x", "c"))),
        check_vma=False,
    )
```

```python
import jax
import jax.numpy as jnp
from jax import lax
from jax.experimental import pallas as pl
from jax.experimental.pallas import tpu as pltpu
from jax.sharding import Mesh
from jax.sharding import PartitionSpec as P

D = 1024
M = 64
K = 256
CENTS = 96
LANES = 128
SUBS = 8
X = 4
Y = 8
ZF = 2
ZS = 6
OWNERS = ("zf", "y")
PEERS = ZF * Y
DP = ("zs", "zf", "y")
DP_SUB = ("zs", "zf", "y", "x", "c")
BOOK0 = D
COARSE0 = D + K
ROWS = D + K + CENTS
GP = D // PEERS
BP = K // PEERS
CP = CENTS // PEERS
C0 = GP + BP
PART = C0 + 16
ONE = PART + BP
SPREAD = C0 + 8
bf16 = jnp.bfloat16
f16 = jnp.float16
f32 = jnp.float32
VMEM = pl.BlockSpec(memory_space=pltpu.VMEM)
SMEM = pl.BlockSpec(memory_space=pltpu.SMEM)
HBM = pl.BlockSpec(memory_space=pltpu.HBM)


def params(mib):
    return pltpu.CompilerParams(vmem_limit_bytes=mib * 2**20)


def dot(a, b):
    return jnp.dot(a, b, preferred_element_type=f32)


def columns(core, x):
    return pl.ds(pl.multiple_of((2 * x + core) * LANES, LANES), LANES)


def residual_sums(e, rot, cent, assigned, codes_of, res, add):
    rows = e.shape[0]
    label = lax.broadcasted_iota(jnp.int32, (CENTS, rows), 0)
    per_zf = CENTS // ZF
    sent = ((label % CP) * ZF + label // per_zf) * Y + (label // CP) % Y
    pick = (label == assigned).astype(bf16)
    send = (sent == assigned).astype(bf16)
    for q in range(X // 2):
        pair = slice(q * 2 * LANES, (q + 1) * 2 * LANES)
        base = lax.dot_general(
            pick, cent[:, pair], (((0,), (0,)), ((), ())), preferred_element_type=f32
        )
        residual = (dot(e[...], rot[:, pair]) - base).astype(bf16)
        res[:, pair] = residual
        coarse = dot(send, residual)
        for k in range(2):
            add(2 * q + k, K, CENTS, coarse[:, k * LANES : (k + 1) * LANES])
    word = lax.broadcasted_iota(jnp.int32, (K, rows), 0)
    lane = lax.broadcasted_iota(jnp.int32, (rows, LANES), 1)

    def book(x, carry):
        codes = codes_of(x)
        mine = res[:, pl.ds(pl.multiple_of(x * LANES, LANES), LANES)]
        total = jnp.zeros((K, LANES), f32)
        for m in range(SUBS):
            onehot = (word == codes[m : m + 1, :]).astype(bf16)
            part = jnp.where(lane // (LANES // SUBS) == m, mine, jnp.zeros_like(mine))
            total += dot(onehot, part)
        add(x, 0, K, total)
        return carry

    lax.fori_loop(0, X, book, 0)


def own_sums(
    core_ref, place_ref, e_in, rot_in, cent_in, codes_in, assigned_in,
    sums, words, e, rot, cent, codes, assigned_ref, res, sems,
):
    core = core_ref[0]
    copies = [
        pltpu.make_async_copy(assigned_in, assigned_ref, sems.at[0]),
        pltpu.make_async_copy(codes_in, codes, sems.at[1]),
        pltpu.make_async_copy(e_in, e, sems.at[2]),
    ]
    for x in range(X):
        here = slice(x * LANES, (x + 1) * LANES)
        for source, target, k in ((cent_in, cent, 0), (rot_in, rot, X)):
            copies.append(
                pltpu.make_async_copy(
                    source.at[:, columns(core, x)], target.at[:, here], sems.at[3 + k + x]
                )
            )
    for copy in copies:
        copy.start()
    for copy in copies:
        copy.wait()
    assigned = assigned_ref[...].reshape(1, -1)

    def rows_of(x, whose):
        return pl.ds(pl.multiple_of((2 * x + whose) * SUBS, SUBS), SUBS)

    for x in range(X):
        words[x * SUBS : (x + 1) * SUBS, :] = codes[rows_of(x, 1 - core), :]
    words[X * SUBS :, :] = jnp.broadcast_to(assigned, (SUBS, assigned.shape[1]))

    def add(x, start, size, value):
        sums[x, start : start + size, :] = value

    residual_sums(e, rot, cent, assigned, lambda x: codes[rows_of(x, core), :], res, add)


def partial_sums(core_ref, e0, e1, rot, cent, words, sums, out, turned, res):
    core = core_ref[0]
    rows = e0.shape[0]
    for x in range(X):
        for h, e in enumerate((e0, e1)):
            turned[x * LANES : (x + 1) * LANES, h * rows : (h + 1) * rows] = e[:, columns(core, x)].T
    wide = 256
    for n in range(D // wide):
        cols = slice(n * wide, (n + 1) * wide)
        g = dot(turned[:, :rows], e0[:, cols]) + dot(turned[:, rows:], e1[:, cols])
        for x in range(X):
            for k in range(wide // LANES):
                j = n * (wide // LANES) + k
                out[x, j * LANES : (j + 1) * LANES, :] = g[
                    x * LANES : (x + 1) * LANES, k * LANES : (k + 1) * LANES
                ].astype(bf16)

    def add(x, start, size, value):
        both = sums[x, start : start + size, :] + value
        out[x, BOOK0 + start : BOOK0 + start + size, :] = both.astype(bf16)

    def codes_of(x):
        return words[pl.ds(pl.multiple_of(x * SUBS, SUBS), SUBS), :]

    assigned = words[X * SUBS : X * SUBS + 1, :]
    residual_sums(e1, rot, cent, assigned, codes_of, res, add)


def first_sums(arrived, out):
    def summed(a, b):
        return arrived[:, a:b, :].astype(f32).sum(axis=0)

    coarse = summed(COARSE0, ROWS)
    zeros = jnp.zeros((PART - C0 - CP, LANES), f32)
    for q in range(PEERS):
        out[q, :GP, :] = summed(q * GP, (q + 1) * GP).astype(bf16)
        out[q, GP:C0, :] = summed(BOOK0 + q * BP, BOOK0 + (q + 1) * BP).astype(bf16)
        mine = coarse[q * CP : (q + 1) * CP, :]
        out[q, C0:PART, :] = jnp.concatenate([mine, zeros], axis=0).astype(bf16)


def second_sums(arrived, out):
    total = arrived[...].astype(f32).sum(axis=0)
    high = total.astype(bf16)
    low = total - high.astype(f32)
    coarse = jnp.concatenate([total[C0 : C0 + 8], low[C0 : C0 + 8]], axis=0).astype(bf16)
    book = low[GP:C0].astype(bf16)
    for i in range(out.shape[0]):
        out[i, :C0, :] = high[:C0]
        out[i, C0:PART, :] = coarse
        out[i, PART:ONE, :] = book


def owned_sums(place_ref, arrived, coarse_out, mine, *, vectors):
    total = arrived[...].astype(f32).sum(axis=0)
    coarse = total[C0 : C0 + 8] + total[C0 + 8 : C0 + 16]
    row = lax.broadcasted_iota(jnp.int32, (8, LANES), 0)
    own = jnp.where(row == place_ref[0], coarse, 0.0).sum(axis=0, keepdims=True)
    coarse_out[...] = own * (CENTS / vectors) ** 0.5
    gram = total[:GP] * (1.0 / vectors)
    book = (total[GP:C0] + total[PART:ONE]) * (K / vectors) ** 0.5

    def scaled(v):
        top = jnp.max(jnp.abs(v), keepdims=True)
        power = jnp.ceil(jnp.log2(jnp.maximum(top, 2.0**-100)))
        return v * jnp.exp2(-power), jnp.broadcast_to(power, (8, LANES))

    gram, gram_power = scaled(gram)
    book, book_power = scaled(book)
    mine[:GP, :] = gram
    mine[GP:C0, :] = book
    mine[C0:SPREAD, :] = jnp.where(row == 0, gram_power, book_power)


def laid_out(arrived, gram, book):
    for q in range(PEERS):
        power = jnp.exp2(arrived[q, C0:SPREAD, :])
        j, top = q * GP // LANES, q * GP % LANES
        gram[top : top + GP, j * LANES : (j + 1) * LANES] = arrived[q, :GP, :] * power[0:1]
        book[q * BP : (q + 1) * BP, :] = arrived[q, GP:C0, :] * power[1:2]


def per_device(embeddings, rotation, centroids, assignments, codes):
    rows = embeddings.shape[0]
    vectors = rows * lax.axis_size(DP_SUB)
    core = lax.axis_index("c").reshape(1)
    place = lax.axis_index("zs").reshape(1)
    swap = [(0, 1), (1, 0)]
    other = lax.ppermute(embeddings, "c", swap)
    half = X * LANES
    sums, words, mine, rotation, centroids = pl.pallas_call(
        own_sums,
        out_shape=(
            jax.ShapeDtypeStruct((X, K + CENTS, LANES), f32),
            jax.ShapeDtypeStruct(((X + 1) * SUBS, rows), jnp.int32),
            jax.ShapeDtypeStruct((rows, D), bf16),
            jax.ShapeDtypeStruct((D, half), bf16),
            jax.ShapeDtypeStruct((CENTS, half), bf16),
        ),
        in_specs=[SMEM] * 2 + [HBM] * 5,
        out_specs=(VMEM,) * 5,
        scratch_shapes=[
            pltpu.VMEM((M, rows), jnp.int32),
            pltpu.VMEM((rows,), jnp.int32),
            pltpu.VMEM((rows, half), bf16),
            pltpu.SemaphoreType.DMA((3 + 2 * X,)),
        ],
        compiler_params=params(24),
        name="own_sums",
    )(core, place, *(pltpu.with_memory_space_constraint(v, pltpu.HBM) for v in (embeddings, rotation, centroids, codes.T, assignments)))
    words = lax.ppermute(words, "c", swap)
    parts = pl.pallas_call(
        partial_sums,
        out_shape=jax.ShapeDtypeStruct((X, ROWS, LANES), bf16),
        in_specs=[SMEM] + [VMEM] * 6,
        out_specs=VMEM,
        scratch_shapes=[pltpu.VMEM((half, 2 * rows), bf16), pltpu.VMEM((rows, half), bf16)],
        compiler_params=params(24),
        name="partial_sums",
    )(core, mine, other, rotation, centroids, words, sums)
    arrived = lax.all_to_all(parts, "x", split_axis=0, concat_axis=0, tiled=True)
    pieces = pl.pallas_call(
        first_sums,
        out_shape=jax.ShapeDtypeStruct((PEERS, PART, LANES), bf16),
        in_specs=[VMEM],
        out_specs=VMEM,
        compiler_params=params(16),
        name="first_sums",
    )(arrived)
    arrived = lax.all_to_all(pieces, OWNERS, split_axis=0, concat_axis=0, tiled=True)
    pieces = pl.pallas_call(
        second_sums,
        out_shape=jax.ShapeDtypeStruct((ZS, ONE, LANES), bf16),
        in_specs=[VMEM],
        out_specs=VMEM,
        compiler_params=params(16),
        name="second_sums",
    )(arrived)
    arrived = lax.all_to_all(pieces, "zs", split_axis=0, concat_axis=0, tiled=True)
    coarse_sums, mine = pl.pallas_call(
        lambda *refs: owned_sums(*refs, vectors=vectors),
        out_shape=(
            jax.ShapeDtypeStruct((1, LANES), f32),
            jax.ShapeDtypeStruct((SPREAD, LANES), f32),
        ),
        in_specs=[SMEM, VMEM],
        out_specs=(VMEM, VMEM),
        compiler_params=params(16),
        name="owned_sums",
    )(place, arrived)
    spread = jnp.broadcast_to(mine.astype(f16)[None], (PEERS, SPREAD, LANES))
    arrived = lax.all_to_all(spread, OWNERS, split_axis=0, concat_axis=0, tiled=True)
    gram, codebook_sums = pl.pallas_call(
        laid_out,
        out_shape=(jax.ShapeDtypeStruct((LANES, D), f32), jax.ShapeDtypeStruct((K, LANES), f32)),
        in_specs=[VMEM],
        out_specs=(VMEM, VMEM),
        compiler_params=params(16),
        name="laid_out",
    )(arrived.astype(f32))
    return gram, coarse_sums, codebook_sums


def solution(mesh):
    finer = Mesh(mesh.devices.reshape(ZS, ZF, Y, X, 2), DP_SUB)
    return jax.shard_map(
        per_device,
        mesh=finer,
        in_specs=(P(DP_SUB, None), P(), P(), P(DP_SUB), P(DP_SUB, None)),
        out_specs=(P(("x", "c"), None), P(DP, ("x", "c")), P(None, ("x", "c"))),
        check_vma=False,
    )
```

```python
import jax
import jax.numpy as jnp
from jax import lax
from jax.experimental import pallas as pl
from jax.experimental.pallas import tpu as pltpu
from jax.sharding import Mesh
from jax.sharding import PartitionSpec as P

D = 1024
M = 64
K = 256
CENTS = 96
LANES = 128
SUBS = 8
X = 4
YS = 4
YF = 2
ZF = 2
ZS = 6
NEAR = ("zf",)
FAR = ("yf", "ys")
PARTS = 2
OWNERS = NEAR + FAR
PEERS = ZF * YF * YS
DP = ("zs", "zf", "ys", "yf")
DP_SUB = ("zs", "zf", "ys", "yf", "x", "c")
BOOK0 = D
COARSE0 = D + K
ROWS = D + K + CENTS
GP = D // PEERS
BP = K // PEERS
CP = CENTS // PEERS
C0 = GP + BP
PART = C0 + 16
ONE = PART + BP
SPREAD = C0 + 8
bf16 = jnp.bfloat16
f16 = jnp.float16
f32 = jnp.float32
VMEM = pl.BlockSpec(memory_space=pltpu.VMEM)
SMEM = pl.BlockSpec(memory_space=pltpu.SMEM)
HBM = pl.BlockSpec(memory_space=pltpu.HBM)


def params(mib):
    return pltpu.CompilerParams(vmem_limit_bytes=mib * 2**20)


def dot(a, b):
    return jnp.dot(a, b, preferred_element_type=f32)


def columns(core, x):
    return pl.ds(pl.multiple_of((2 * x + core) * LANES, LANES), LANES)


def residual_sums(e, rot, cent, assigned, codes, res):
    rows = e.shape[0]
    label = lax.broadcasted_iota(jnp.int32, (CENTS, rows), 0)
    owner = label // CP
    zf, yf, ys = owner // (YF * YS), owner // YS % YF, owner % YS
    sent = (((label % CP) * ZF + zf) * YS + ys) * YF + yf
    pick = (label == assigned).astype(bf16)
    send = (sent == assigned).astype(bf16)
    coarse = []
    for q in range(X // 2):
        pair = slice(q * 2 * LANES, (q + 1) * 2 * LANES)
        base = lax.dot_general(
            pick, cent[:, pair], (((0,), (0,)), ((), ())), preferred_element_type=f32
        )
        residual = (dot(e[...], rot[:, pair]) - base).astype(bf16)
        res[:, pair] = residual
        coarse.append(dot(send, residual))
    return coarse


def book_sums(res, codes):
    rows = res.shape[0]
    word = lax.broadcasted_iota(jnp.int32, (K, rows), 0)
    lane = lax.broadcasted_iota(jnp.int32, (rows, LANES), 1)
    total = jnp.zeros((K, LANES), f32)
    for m in range(SUBS):
        onehot = (word == codes[m : m + 1, :]).astype(bf16)
        part = jnp.where(lane // (LANES // SUBS) == m, res, jnp.zeros_like(res))
        total += dot(onehot, part)
    return total


def other_words(core_ref, place_ref, codes_in, assigned_in, words, assigned, sems):
    core = core_ref[0]
    copies = [pltpu.make_async_copy(assigned_in, assigned, sems.at[X])]
    for x in range(X):
        theirs = pl.ds(pl.multiple_of((2 * x + 1 - core) * SUBS, SUBS), SUBS)
        copies.append(
            pltpu.make_async_copy(
                codes_in.at[theirs, :], words.at[x * SUBS : (x + 1) * SUBS, :], sems.at[x]
            )
        )
    for copy in copies:
        copy.start()
    for copy in copies:
        copy.wait()
    words[X * SUBS :, :] = jnp.broadcast_to(assigned[...].reshape(1, -1), (SUBS, words.shape[1]))


def partial_sums(
    core_ref, e_in, rot_in, cent_in, codes_in, assigned_in, e1, words,
    out, e0, rot, cent, codes, assigned_ref, turned, res, sems,
):
    core = core_ref[0]
    rows = e1.shape[0]
    first = pltpu.make_async_copy(e_in, e0, sems.at[0])
    first.start()
    copies = [pltpu.make_async_copy(assigned_in, assigned_ref, sems.at[1])]
    for x in range(X):
        here = slice(x * LANES, (x + 1) * LANES)
        lanes = columns(core, x)
        mine = pl.ds(pl.multiple_of((2 * x + core) * SUBS, SUBS), SUBS)
        copies += [
            pltpu.make_async_copy(rot_in.at[:, lanes], rot.at[:, here], sems.at[2 + 3 * x]),
            pltpu.make_async_copy(cent_in.at[:, lanes], cent.at[:, here], sems.at[3 + 3 * x]),
            pltpu.make_async_copy(
                codes_in.at[mine, :], codes.at[x * SUBS : (x + 1) * SUBS, :], sems.at[4 + 3 * x]
            ),
        ]
    for copy in copies:
        copy.start()
    for x in range(X):
        turned[x * LANES : (x + 1) * LANES, rows:] = e1[:, columns(core, x)].T
    first.wait()
    for x in range(X):
        turned[x * LANES : (x + 1) * LANES, :rows] = e0[:, columns(core, x)].T
    wide = 256
    grams = D // PARTS
    for n in range(D // wide):
        cols = slice(n * wide, (n + 1) * wide)
        g = dot(turned[:, :rows], e0[:, cols]) + dot(turned[:, rows:], e1[:, cols])
        for x in range(X):
            for k in range(wide // LANES):
                part, row = divmod((n * (wide // LANES) + k) * LANES, grams)
                out[part, x, row : row + LANES, :] = g[
                    x * LANES : (x + 1) * LANES, k * LANES : (k + 1) * LANES
                ].astype(bf16)
    for copy in copies:
        copy.wait()
    own = residual_sums(e0, rot, cent, assigned_ref[...].reshape(1, -1), codes, res.at[:rows])
    theirs = residual_sums(e1, rot, cent, words[X * SUBS : X * SUBS + 1, :], words, res.at[rows:])
    books, cents = K // PARTS, CENTS // PARTS
    book0, coarse0 = grams, grams + books
    for q in range(X // 2):
        coarse = (own[q] + theirs[q]).astype(bf16)
        for k in range(2):
            for part in range(PARTS):
                piece = coarse[part * cents : (part + 1) * cents, k * LANES : (k + 1) * LANES]
                out[part, 2 * q + k, coarse0:, :] = piece

    for x in range(X):
        subs = slice(x * SUBS, (x + 1) * SUBS)
        lanes = slice(x * LANES, (x + 1) * LANES)
        total = book_sums(res[:rows, lanes], codes[subs, :])
        total = (total + book_sums(res[rows:, lanes], words[subs, :])).astype(bf16)
        for part in range(PARTS):
            out[part, x, book0:coarse0, :] = total[part * books : (part + 1) * books]
def first_sums(arrived, out):
    def summed(a, b):
        return arrived[:, a:b, :].astype(f32).sum(axis=0)

    grams, books = D // PARTS, K // PARTS
    coarse = summed(grams + books, ROWS // PARTS)
    zeros = jnp.zeros((PART - C0 - CP, LANES), f32)
    for q in range(out.shape[0]):
        out[q, :GP, :] = summed(q * GP, (q + 1) * GP).astype(bf16)
        out[q, GP:C0, :] = summed(grams + q * BP, grams + (q + 1) * BP).astype(bf16)
        mine = coarse[q * CP : (q + 1) * CP, :]
        out[q, C0:PART, :] = jnp.concatenate([mine, zeros], axis=0).astype(bf16)


def second_sums(arrived, out):
    total = arrived[...].astype(f32).sum(axis=0)
    high = total.astype(bf16)
    low = total - high.astype(f32)
    coarse = jnp.concatenate([total[C0 : C0 + 8], low[C0 : C0 + 8]], axis=0).astype(bf16)
    book = low[GP:C0].astype(bf16)
    for i in range(out.shape[0]):
        out[i, :C0, :] = high[:C0]
        out[i, C0:PART, :] = coarse
        out[i, PART:ONE, :] = book


def owned_sums(place_ref, arrived, coarse_out, mine, *, vectors):
    total = arrived[...].astype(f32).sum(axis=0)
    coarse = total[C0 : C0 + 8] + total[C0 + 8 : C0 + 16]
    row = lax.broadcasted_iota(jnp.int32, (8, LANES), 0)
    own = jnp.where(row == place_ref[0], coarse, 0.0).sum(axis=0, keepdims=True)
    coarse_out[...] = own * (CENTS / vectors) ** 0.5
    gram = total[:GP] * (1.0 / vectors)
    book = (total[GP:C0] + total[PART:ONE]) * (K / vectors) ** 0.5

    def scaled(v):
        top = jnp.max(jnp.abs(v), keepdims=True)
        power = jnp.ceil(jnp.log2(jnp.maximum(top, 2.0**-100)))
        return v * jnp.exp2(-power), jnp.broadcast_to(power, (8, LANES))

    gram, gram_power = scaled(gram)
    book, book_power = scaled(book)
    mine[:GP, :] = gram
    mine[GP:C0, :] = book
    mine[C0:SPREAD, :] = jnp.where(row == 0, gram_power, book_power)


def laid_out(arrived, gram, book):
    for q in range(PEERS):
        power = jnp.exp2(arrived[q, C0:SPREAD, :])
        j, top = q * GP // LANES, q * GP % LANES
        gram[top : top + GP, j * LANES : (j + 1) * LANES] = arrived[q, :GP, :] * power[0:1]
        book[q * BP : (q + 1) * BP, :] = arrived[q, GP:C0, :] * power[1:2]


def per_device(embeddings, rotation, centroids, assignments, codes):
    rows = embeddings.shape[0]
    vectors = rows * lax.axis_size(DP_SUB)
    core = lax.axis_index("c").reshape(1)
    place = lax.axis_index("zs").reshape(1)
    swap = [(0, 1), (1, 0)]
    other = lax.ppermute(embeddings, "c", swap)
    half = X * LANES
    inputs = (embeddings, rotation, centroids, codes.T, assignments)
    inputs = tuple(pltpu.with_memory_space_constraint(v, pltpu.HBM) for v in inputs)
    words = pl.pallas_call(
        other_words,
        out_shape=jax.ShapeDtypeStruct(((X + 1) * SUBS, rows), jnp.int32),
        in_specs=[SMEM] * 2 + [HBM] * 2,
        out_specs=VMEM,
        scratch_shapes=[pltpu.VMEM((rows,), jnp.int32), pltpu.SemaphoreType.DMA((X + 1,))],
        compiler_params=params(16),
        name="other_words",
    )(core, place, *inputs[3:])
    words = lax.ppermute(words, "c", swap)
    parts = pl.pallas_call(
        partial_sums,
        out_shape=jax.ShapeDtypeStruct((PARTS, X, ROWS // PARTS, LANES), bf16),
        in_specs=[SMEM] + [HBM] * 5 + [VMEM] * 2,
        out_specs=VMEM,
        scratch_shapes=[
            pltpu.VMEM((rows, D), bf16),
            pltpu.VMEM((D, half), bf16),
            pltpu.VMEM((CENTS, half), bf16),
            pltpu.VMEM((X * SUBS, rows), jnp.int32),
            pltpu.VMEM((rows,), jnp.int32),
            pltpu.VMEM((half, 2 * rows), bf16),
            pltpu.VMEM((2 * rows, half), bf16),
            pltpu.SemaphoreType.DMA((2 + 3 * X,)),
        ],
        compiler_params=params(32),
        name="partial_sums",
    )(core, *inputs, other, words)
    parts = parts.reshape(PARTS * X, ROWS // PARTS, LANES)
    arrived = lax.all_to_all(parts, NEAR + ("x",), split_axis=0, concat_axis=0, tiled=True)
    pieces = pl.pallas_call(
        first_sums,
        out_shape=jax.ShapeDtypeStruct((PEERS // PARTS, PART, LANES), bf16),
        in_specs=[VMEM],
        out_specs=VMEM,
        compiler_params=params(16),
        name="first_sums",
    )(arrived)
    arrived = lax.all_to_all(pieces, FAR, split_axis=0, concat_axis=0, tiled=True)
    pieces = pl.pallas_call(
        second_sums,
        out_shape=jax.ShapeDtypeStruct((ZS, ONE, LANES), bf16),
        in_specs=[VMEM],
        out_specs=VMEM,
        compiler_params=params(16),
        name="second_sums",
    )(arrived)
    arrived = lax.all_to_all(pieces, "zs", split_axis=0, concat_axis=0, tiled=True)
    coarse_sums, mine = pl.pallas_call(
        lambda *refs: owned_sums(*refs, vectors=vectors),
        out_shape=(
            jax.ShapeDtypeStruct((1, LANES), f32),
            jax.ShapeDtypeStruct((SPREAD, LANES), f32),
        ),
        in_specs=[SMEM, VMEM],
        out_specs=(VMEM, VMEM),
        compiler_params=params(16),
        name="owned_sums",
    )(place, arrived)
    spread = jnp.broadcast_to(mine.astype(f16)[None], (PEERS, SPREAD, LANES))
    arrived = lax.all_to_all(spread, OWNERS, split_axis=0, concat_axis=0, tiled=True)
    gram, codebook_sums = pl.pallas_call(
        laid_out,
        out_shape=(jax.ShapeDtypeStruct((LANES, D), f32), jax.ShapeDtypeStruct((K, LANES), f32)),
        in_specs=[VMEM],
        out_specs=(VMEM, VMEM),
        compiler_params=params(16),
        name="laid_out",
    )(arrived.astype(f32))
    return gram, coarse_sums, codebook_sums


def solution(mesh):
    finer = Mesh(mesh.devices.reshape(ZS, ZF, YS, YF, X, 2), DP_SUB)
    return jax.shard_map(
        per_device,
        mesh=finer,
        in_specs=(P(DP_SUB, None), P(), P(), P(DP_SUB), P(DP_SUB, None)),
        out_specs=(P(("x", "c"), None), P(DP, ("x", "c")), P(None, ("x", "c"))),
        check_vma=False,
    )
```

```python
import jax
import jax.numpy as jnp
from jax import lax
from jax.experimental import pallas as pl
from jax.experimental.pallas import tpu as pltpu
from jax.sharding import Mesh
from jax.sharding import PartitionSpec as P

D = 1024
M = 64
K = 256
CENTS = 96
LANES = 128
SUBS = 8
X = 4
YS = 4
YF = 2
ZF = 2
ZS = 6
NEAR = ("zf",)
FAR = ("yf", "ys")
PARTS = 2
OWNERS = NEAR + FAR
PEERS = ZF * YF * YS
DP = ("zs", "zf", "ys", "yf")
DP_SUB = ("zs", "zf", "ys", "yf", "x", "c")
BOOK0 = D
COARSE0 = D + K
ROWS = D + K + CENTS
GP = D // PEERS
BP = K // PEERS
CP = CENTS // PEERS
C0 = GP + BP
PART = C0 + 16
ONE = PART + BP
SPREAD = C0 + 8
bf16 = jnp.bfloat16
f16 = jnp.float16
f32 = jnp.float32
VMEM = pl.BlockSpec(memory_space=pltpu.VMEM)
SMEM = pl.BlockSpec(memory_space=pltpu.SMEM)
HBM = pl.BlockSpec(memory_space=pltpu.HBM)


def params(mib):
    return pltpu.CompilerParams(vmem_limit_bytes=mib * 2**20)


def dot(a, b):
    return jnp.dot(a, b, preferred_element_type=f32)


def columns(core, x):
    return pl.ds(pl.multiple_of((2 * x + core) * LANES, LANES), LANES)


def book_sums(res, codes):
    rows = res.shape[0]
    word = lax.broadcasted_iota(jnp.int32, (K, rows), 0)
    lane = lax.broadcasted_iota(jnp.int32, (rows, LANES), 1)
    total = jnp.zeros((K, LANES), f32)
    for m in range(SUBS):
        onehot = (word == codes[m : m + 1, :]).astype(bf16)
        part = jnp.where(lane // (LANES // SUBS) == m, res, jnp.zeros_like(res))
        total += dot(onehot, part)
    return total


def half_sums(whose, e, rot, cent, codes, assigned, out, turned, wait=None):
    rows = e.shape[0]
    for x in range(X):
        turned[x * LANES : (x + 1) * LANES, :] = e[:, columns(whose, x)].T
    wide = 256
    grams, books, cents = D // PARTS, K // PARTS, CENTS // PARTS
    book0, coarse0 = grams, grams + books
    for n in range(D // wide):
        g = dot(turned[...], e[:, n * wide : (n + 1) * wide])
        for x in range(X):
            for k in range(wide // LANES):
                part, row = divmod((n * (wide // LANES) + k) * LANES, grams)
                out[part, x, row : row + LANES, :] = g[
                    x * LANES : (x + 1) * LANES, k * LANES : (k + 1) * LANES
                ].astype(out.dtype)
    if wait is not None:
        wait()
    label = lax.broadcasted_iota(jnp.int32, (CENTS, rows), 0)
    owner = label // CP
    zf, yf, ys = owner // (YF * YS), owner // YS % YF, owner % YS
    sent = (((label % CP) * ZF + zf) * YS + ys) * YF + yf
    named = assigned[...].reshape(1, rows)
    pick = (label == named).astype(bf16)
    send = (sent == named).astype(bf16)
    for q in range(X // 2):
        pair = (columns(whose, 2 * q), columns(whose, 2 * q + 1))
        c = jnp.concatenate([cent[:, p] for p in pair], axis=1)
        r = jnp.concatenate([rot[:, p] for p in pair], axis=1)
        base = lax.dot_general(pick, c, (((0,), (0,)), ((), ())), preferred_element_type=f32)
        residual = (dot(e[...], r) - base).astype(bf16)
        coarse = dot(send, residual).astype(out.dtype)
        for k in range(2):
            x = 2 * q + k
            lanes = slice(k * LANES, (k + 1) * LANES)
            subs = pl.ds(pl.multiple_of((2 * x + whose) * SUBS, SUBS), SUBS)
            total = book_sums(residual[:, lanes], codes[subs, :]).astype(out.dtype)
            for part in range(PARTS):
                out[part, x, book0:coarse0, :] = total[part * books : (part + 1) * books]
                out[part, x, coarse0:, :] = coarse[part * cents : (part + 1) * cents, lanes]


def sibling_sums(
    core_ref, place_ref, e_in, rot_in, cent_in, codes_in, assigned_in,
    out, e, rot, cent, codes, assigned, turned, sems,
):
    pairs = (
        (e_in, e), (assigned_in, assigned), (cent_in, cent), (codes_in, codes), (rot_in, rot),
    )
    copies = [pltpu.make_async_copy(a, b, sems.at[i]) for i, (a, b) in enumerate(pairs)]
    for copy in copies:
        copy.start()
    copies[0].wait()

    def wait():
        for copy in copies[1:]:
            copy.wait()

    half_sums(1 - core_ref[0], e, rot, cent, codes, assigned, out, turned, wait)


def own_sums(core_ref, e, rot, cent, codes, assigned, out, turned):
    half_sums(core_ref[0], e, rot, cent, codes, assigned, out, turned)


def chip_sums(mine, theirs, out):
    for part in range(mine.shape[0]):

        def add(x, carry):
            out[part, x] = (mine[part, x] + theirs[part, x].astype(f32)).astype(bf16)
            return carry

        lax.fori_loop(0, X, add, 0)


def first_sums(arrived, out):
    def summed(a, b):
        return arrived[:, a:b, :].astype(f32).sum(axis=0)

    grams, books = D // PARTS, K // PARTS
    coarse = summed(grams + books, ROWS // PARTS)
    zeros = jnp.zeros((PART - C0 - CP, LANES), f32)
    for q in range(out.shape[0]):
        out[q, :GP, :] = summed(q * GP, (q + 1) * GP).astype(bf16)
        out[q, GP:C0, :] = summed(grams + q * BP, grams + (q + 1) * BP).astype(bf16)
        mine = coarse[q * CP : (q + 1) * CP, :]
        out[q, C0:PART, :] = jnp.concatenate([mine, zeros], axis=0).astype(bf16)


def second_sums(arrived, out):
    total = arrived[...].astype(f32).sum(axis=0)
    high = total.astype(bf16)
    low = total - high.astype(f32)
    coarse = jnp.concatenate([total[C0 : C0 + 8], low[C0 : C0 + 8]], axis=0).astype(bf16)
    book = low[GP:C0].astype(bf16)
    for i in range(out.shape[0]):
        out[i, :C0, :] = high[:C0]
        out[i, C0:PART, :] = coarse
        out[i, PART:ONE, :] = book


def owned_sums(place_ref, arrived, coarse_out, mine, *, vectors):
    total = arrived[...].astype(f32).sum(axis=0)
    coarse = total[C0 : C0 + 8] + total[C0 + 8 : C0 + 16]
    row = lax.broadcasted_iota(jnp.int32, (8, LANES), 0)
    own = jnp.where(row == place_ref[0], coarse, 0.0).sum(axis=0, keepdims=True)
    coarse_out[...] = own * (CENTS / vectors) ** 0.5
    gram = total[:GP] * (1.0 / vectors)
    book = (total[GP:C0] + total[PART:ONE]) * (K / vectors) ** 0.5

    def scaled(v):
        top = jnp.max(jnp.abs(v), keepdims=True)
        power = jnp.ceil(jnp.log2(jnp.maximum(top, 2.0**-100)))
        return v * jnp.exp2(-power), jnp.broadcast_to(power, (8, LANES))

    gram, gram_power = scaled(gram)
    book, book_power = scaled(book)
    mine[:GP, :] = gram
    mine[GP:C0, :] = book
    mine[C0:SPREAD, :] = jnp.where(row == 0, gram_power, book_power)


def laid_out(arrived, gram, book):
    for q in range(PEERS):
        power = jnp.exp2(arrived[q, C0:SPREAD, :])
        j, top = q * GP // LANES, q * GP % LANES
        gram[top : top + GP, j * LANES : (j + 1) * LANES] = arrived[q, :GP, :] * power[0:1]
        book[q * BP : (q + 1) * BP, :] = arrived[q, GP:C0, :] * power[1:2]


def per_device(embeddings, rotation, centroids, assignments, codes):
    rows = embeddings.shape[0]
    vectors = rows * lax.axis_size(DP_SUB)
    core = lax.axis_index("c").reshape(1)
    place = lax.axis_index("zs").reshape(1)
    inputs = (embeddings, rotation, centroids, codes.T, assignments)
    inputs = tuple(pltpu.with_memory_space_constraint(v, pltpu.HBM) for v in inputs)
    shape = (PARTS, X, ROWS // PARTS, LANES)
    turned = pltpu.VMEM((X * LANES, rows), bf16)
    theirs, *held = pl.pallas_call(
        sibling_sums,
        out_shape=[jax.ShapeDtypeStruct(shape, bf16)]
        + [jax.ShapeDtypeStruct(v.shape, v.dtype) for v in inputs],
        in_specs=[SMEM] * 2 + [HBM] * 5,
        out_specs=[VMEM] * 6,
        scratch_shapes=[turned, pltpu.SemaphoreType.DMA((5,))],
        compiler_params=params(24),
        name="sibling_sums",
    )(core, place, *inputs)
    arrived = lax.ppermute(theirs, "c", [(0, 1), (1, 0)])
    mine = pl.pallas_call(
        own_sums,
        out_shape=jax.ShapeDtypeStruct(shape, f32),
        in_specs=[SMEM] + [VMEM] * 5,
        out_specs=VMEM,
        scratch_shapes=[turned],
        compiler_params=params(24),
        cost_estimate=pl.CostEstimate(flops=4 * 10**9, bytes_accessed=8 * 10**6, transcendentals=0),
        name="own_sums",
    )(core, *held)
    parts = pl.pallas_call(
        chip_sums,
        out_shape=jax.ShapeDtypeStruct(shape, bf16),
        in_specs=[VMEM] * 2,
        out_specs=VMEM,
        compiler_params=params(16),
        name="chip_sums",
    )(mine, arrived)
    parts = parts.reshape(PARTS * X, ROWS // PARTS, LANES)
    arrived = lax.all_to_all(parts, NEAR + ("x",), split_axis=0, concat_axis=0, tiled=True)
    pieces = pl.pallas_call(
        first_sums,
        out_shape=jax.ShapeDtypeStruct((PEERS // PARTS, PART, LANES), bf16),
        in_specs=[VMEM],
        out_specs=VMEM,
        compiler_params=params(16),
        name="first_sums",
    )(arrived)
    arrived = lax.all_to_all(pieces, FAR, split_axis=0, concat_axis=0, tiled=True)
    pieces = pl.pallas_call(
        second_sums,
        out_shape=jax.ShapeDtypeStruct((ZS, ONE, LANES), bf16),
        in_specs=[VMEM],
        out_specs=VMEM,
        compiler_params=params(16),
        name="second_sums",
    )(arrived)
    arrived = lax.all_to_all(pieces, "zs", split_axis=0, concat_axis=0, tiled=True)
    coarse_sums, mine = pl.pallas_call(
        lambda *refs: owned_sums(*refs, vectors=vectors),
        out_shape=(
            jax.ShapeDtypeStruct((1, LANES), f32),
            jax.ShapeDtypeStruct((SPREAD, LANES), f32),
        ),
        in_specs=[SMEM, VMEM],
        out_specs=(VMEM, VMEM),
        compiler_params=params(16),
        name="owned_sums",
    )(place, arrived)
    spread = jnp.broadcast_to(mine.astype(f16)[None], (PEERS, SPREAD, LANES))
    arrived = lax.all_to_all(spread, OWNERS, split_axis=0, concat_axis=0, tiled=True)
    gram, codebook_sums = pl.pallas_call(
        laid_out,
        out_shape=(jax.ShapeDtypeStruct((LANES, D), f32), jax.ShapeDtypeStruct((K, LANES), f32)),
        in_specs=[VMEM],
        out_specs=(VMEM, VMEM),
        compiler_params=params(16),
        name="laid_out",
    )(arrived.astype(f32))
    return gram, coarse_sums, codebook_sums


def solution(mesh):
    finer = Mesh(mesh.devices.reshape(ZS, ZF, YS, YF, X, 2), DP_SUB)
    return jax.shard_map(
        per_device,
        mesh=finer,
        in_specs=(P(DP_SUB, None), P(), P(), P(DP_SUB), P(DP_SUB, None)),
        out_specs=(P(("x", "c"), None), P(DP, ("x", "c")), P(None, ("x", "c"))),
        check_vma=False,
    )
```

```python
import jax
import jax.numpy as jnp
from jax import lax
from jax.experimental import pallas as pl
from jax.experimental.pallas import tpu as pltpu
from jax.sharding import Mesh
from jax.sharding import PartitionSpec as P

D = 1024
M = 64
K = 256
CENTS = 96
LANES = 128
SUBS = 8
GROUPS = 4
X = 4
YS = 4
YF = 2
ZF = 2
ZS = 6
NEAR = ("zf",)
FAR = ("yf", "ys")
PARTS = 2
OWNERS = NEAR + FAR
PEERS = ZF * YF * YS
DP = ("zs", "zf", "ys", "yf")
DP_SUB = ("zs", "zf", "ys", "yf", "x", "c")
BOOK0 = D
COARSE0 = D + K
ROWS = D + K + CENTS
GP = D // PEERS
BP = K // PEERS
CP = CENTS // PEERS
C0 = GP + BP
PART = C0 + 16
ONE = PART + BP
SPREAD = C0 + 8
bf16 = jnp.bfloat16
f16 = jnp.float16
f32 = jnp.float32
VMEM = pl.BlockSpec(memory_space=pltpu.VMEM)
SMEM = pl.BlockSpec(memory_space=pltpu.SMEM)
HBM = pl.BlockSpec(memory_space=pltpu.HBM)


def params(mib):
    return pltpu.CompilerParams(vmem_limit_bytes=mib * 2**20)


def dot(a, b):
    return jnp.dot(a, b, preferred_element_type=f32)


def columns(core, x):
    return pl.ds(pl.multiple_of((2 * x + core) * LANES, LANES), LANES)


def book_sums(res, codes):
    rows = res.shape[0]
    low_words = K // GROUPS
    group = lax.shift_right_logical(codes, low_words.bit_length() - 1)
    low = codes - group * low_words
    sub = lax.broadcasted_iota(jnp.int32, (SUBS, LANES), 0)
    lane = lax.broadcasted_iota(jnp.int32, (SUBS, LANES), 1)
    select = (lane // (LANES // SUBS) == sub).astype(f32).astype(bf16)
    group = group.astype(f32).astype(bf16)
    which = lax.dot_general(group, select, (((0,), (0,)), ((), ())), preferred_element_type=f32)
    zeros = jnp.zeros_like(res)
    spread = jnp.concatenate([jnp.where(which == g, res, zeros) for g in range(GROUPS)], axis=1)
    word = lax.broadcasted_iota(jnp.int32, (low_words, rows), 0)
    onehot = [(word == low[m : m + 1, :]).astype(bf16) for m in range(SUBS)]
    sums = dot(jnp.concatenate(onehot, axis=0), spread)
    mine = lax.broadcasted_iota(jnp.int32, (low_words, LANES), 1) // (LANES // SUBS)
    totals = []
    for g in range(GROUPS):
        total = jnp.zeros((low_words, LANES), f32)
        for m in range(SUBS):
            part = sums[m * low_words : (m + 1) * low_words, g * LANES : (g + 1) * LANES]
            total = jnp.where(mine == m, part, total)
        totals.append(total)
    return jnp.concatenate(totals, axis=0)


def half_sums(whose, e, rot, cent, codes, assigned, out, turned, wait=None):
    rows = e.shape[0]
    for x in range(X):
        turned[x * LANES : (x + 1) * LANES, :] = e[:, columns(whose, x)].T
    wide = 256
    grams, books, cents = D // PARTS, K // PARTS, CENTS // PARTS
    book0, coarse0 = grams, grams + books
    for n in range(D // wide):
        g = dot(turned[...], e[:, n * wide : (n + 1) * wide])
        for x in range(X):
            for k in range(wide // LANES):
                part, row = divmod((n * (wide // LANES) + k) * LANES, grams)
                out[part, x, row : row + LANES, :] = g[
                    x * LANES : (x + 1) * LANES, k * LANES : (k + 1) * LANES
                ].astype(out.dtype)
    if wait is not None:
        wait()
    label = lax.broadcasted_iota(jnp.int32, (CENTS, rows), 0)
    owner = label // CP
    zf, yf, ys = owner // (YF * YS), owner // YS % YF, owner % YS
    sent = (((label % CP) * ZF + zf) * YS + ys) * YF + yf
    named = assigned[...].reshape(1, rows)
    pick = (label == named).astype(bf16)
    send = (sent == named).astype(bf16)
    for q in range(X // 2):
        pair = (columns(whose, 2 * q), columns(whose, 2 * q + 1))
        c = jnp.concatenate([cent[:, p] for p in pair], axis=1)
        r = jnp.concatenate([rot[:, p] for p in pair], axis=1)
        base = lax.dot_general(pick, c, (((0,), (0,)), ((), ())), preferred_element_type=f32)
        residual = (dot(e[...], r) - base).astype(bf16)
        coarse = dot(send, residual).astype(out.dtype)
        for k in range(2):
            x = 2 * q + k
            lanes = slice(k * LANES, (k + 1) * LANES)
            subs = pl.ds(pl.multiple_of((2 * x + whose) * SUBS, SUBS), SUBS)
            total = book_sums(residual[:, lanes], codes[subs, :]).astype(out.dtype)
            for part in range(PARTS):
                out[part, x, book0:coarse0, :] = total[part * books : (part + 1) * books]
                out[part, x, coarse0:, :] = coarse[part * cents : (part + 1) * cents, lanes]


def sibling_sums(
    core_ref, place_ref, e_in, rot_in, cent_in, codes_in, assigned_in,
    out, e, rot, cent, codes, assigned, turned, sems,
):
    pairs = (
        (e_in, e), (assigned_in, assigned), (cent_in, cent), (codes_in, codes), (rot_in, rot),
    )
    copies = [pltpu.make_async_copy(a, b, sems.at[i]) for i, (a, b) in enumerate(pairs)]
    for copy in copies:
        copy.start()
    copies[0].wait()

    def wait():
        for copy in copies[1:]:
            copy.wait()

    half_sums(1 - core_ref[0], e, rot, cent, codes, assigned, out, turned, wait)


def own_sums(core_ref, e, rot, cent, codes, assigned, out, turned):
    half_sums(core_ref[0], e, rot, cent, codes, assigned, out, turned)


def chip_sums(mine, theirs, out):
    for part in range(mine.shape[0]):

        def add(x, carry):
            out[part, x] = (mine[part, x] + theirs[part, x].astype(f32)).astype(bf16)
            return carry

        lax.fori_loop(0, X, add, 0)


def first_sums(arrived, out):
    def summed(a, b):
        return arrived[:, a:b, :].astype(f32).sum(axis=0)

    grams, books = D // PARTS, K // PARTS
    coarse = summed(grams + books, ROWS // PARTS)
    zeros = jnp.zeros((PART - C0 - CP, LANES), f32)
    for q in range(out.shape[0]):
        out[q, :GP, :] = summed(q * GP, (q + 1) * GP).astype(bf16)
        out[q, GP:C0, :] = summed(grams + q * BP, grams + (q + 1) * BP).astype(bf16)
        mine = coarse[q * CP : (q + 1) * CP, :]
        out[q, C0:PART, :] = jnp.concatenate([mine, zeros], axis=0).astype(bf16)


def second_sums(arrived, out):
    total = arrived[...].astype(f32).sum(axis=0)
    high = total.astype(bf16)
    low = total - high.astype(f32)
    coarse = jnp.concatenate([total[C0 : C0 + 8], low[C0 : C0 + 8]], axis=0).astype(bf16)
    book = low[GP:C0].astype(bf16)
    for i in range(out.shape[0]):
        out[i, :C0, :] = high[:C0]
        out[i, C0:PART, :] = coarse
        out[i, PART:ONE, :] = book


def owned_sums(place_ref, arrived, coarse_out, mine, *, vectors):
    total = arrived[...].astype(f32).sum(axis=0)
    coarse = total[C0 : C0 + 8] + total[C0 + 8 : C0 + 16]
    row = lax.broadcasted_iota(jnp.int32, (8, LANES), 0)
    own = jnp.where(row == place_ref[0], coarse, 0.0).sum(axis=0, keepdims=True)
    coarse_out[...] = own * (CENTS / vectors) ** 0.5
    gram = total[:GP] * (1.0 / vectors)
    book = (total[GP:C0] + total[PART:ONE]) * (K / vectors) ** 0.5

    def scaled(v):
        top = jnp.max(jnp.abs(v), keepdims=True)
        power = jnp.ceil(jnp.log2(jnp.maximum(top, 2.0**-100)))
        return v * jnp.exp2(-power), jnp.broadcast_to(power, (8, LANES))

    gram, gram_power = scaled(gram)
    book, book_power = scaled(book)
    mine[:GP, :] = gram
    mine[GP:C0, :] = book
    mine[C0:SPREAD, :] = jnp.where(row == 0, gram_power, book_power)


def laid_out(arrived, gram, book):
    for q in range(PEERS):
        power = jnp.exp2(arrived[q, C0:SPREAD, :])
        j, top = q * GP // LANES, q * GP % LANES
        gram[top : top + GP, j * LANES : (j + 1) * LANES] = arrived[q, :GP, :] * power[0:1]
        book[q * BP : (q + 1) * BP, :] = arrived[q, GP:C0, :] * power[1:2]


def per_device(embeddings, rotation, centroids, assignments, codes):
    rows = embeddings.shape[0]
    vectors = rows * lax.axis_size(DP_SUB)
    core = lax.axis_index("c").reshape(1)
    place = lax.axis_index("zs").reshape(1)
    inputs = (embeddings, rotation, centroids, codes.T, assignments)
    inputs = tuple(pltpu.with_memory_space_constraint(v, pltpu.HBM) for v in inputs)
    shape = (PARTS, X, ROWS // PARTS, LANES)
    turned = pltpu.VMEM((X * LANES, rows), bf16)
    theirs, *held = pl.pallas_call(
        sibling_sums,
        out_shape=[jax.ShapeDtypeStruct(shape, bf16)]
        + [jax.ShapeDtypeStruct(v.shape, v.dtype) for v in inputs],
        in_specs=[SMEM] * 2 + [HBM] * 5,
        out_specs=[VMEM] * 6,
        scratch_shapes=[turned, pltpu.SemaphoreType.DMA((5,))],
        compiler_params=params(24),
        name="sibling_sums",
    )(core, place, *inputs)
    arrived = lax.ppermute(theirs, "c", [(0, 1), (1, 0)])
    mine = pl.pallas_call(
        own_sums,
        out_shape=jax.ShapeDtypeStruct(shape, f32),
        in_specs=[SMEM] + [VMEM] * 5,
        out_specs=VMEM,
        scratch_shapes=[turned],
        compiler_params=params(24),
        cost_estimate=pl.CostEstimate(flops=4 * 10**9, bytes_accessed=8 * 10**6, transcendentals=0),
        name="own_sums",
    )(core, *held)
    parts = pl.pallas_call(
        chip_sums,
        out_shape=jax.ShapeDtypeStruct(shape, bf16),
        in_specs=[VMEM] * 2,
        out_specs=VMEM,
        compiler_params=params(16),
        name="chip_sums",
    )(mine, arrived)
    parts = parts.reshape(PARTS * X, ROWS // PARTS, LANES)
    arrived = lax.all_to_all(parts, NEAR + ("x",), split_axis=0, concat_axis=0, tiled=True)
    pieces = pl.pallas_call(
        first_sums,
        out_shape=jax.ShapeDtypeStruct((PEERS // PARTS, PART, LANES), bf16),
        in_specs=[VMEM],
        out_specs=VMEM,
        compiler_params=params(16),
        name="first_sums",
    )(arrived)
    arrived = lax.all_to_all(pieces, FAR, split_axis=0, concat_axis=0, tiled=True)
    pieces = pl.pallas_call(
        second_sums,
        out_shape=jax.ShapeDtypeStruct((ZS, ONE, LANES), bf16),
        in_specs=[VMEM],
        out_specs=VMEM,
        compiler_params=params(16),
        name="second_sums",
    )(arrived)
    arrived = lax.all_to_all(pieces, "zs", split_axis=0, concat_axis=0, tiled=True)
    coarse_sums, mine = pl.pallas_call(
        lambda *refs: owned_sums(*refs, vectors=vectors),
        out_shape=(
            jax.ShapeDtypeStruct((1, LANES), f32),
            jax.ShapeDtypeStruct((SPREAD, LANES), f32),
        ),
        in_specs=[SMEM, VMEM],
        out_specs=(VMEM, VMEM),
        compiler_params=params(16),
        name="owned_sums",
    )(place, arrived)
    spread = jnp.broadcast_to(mine.astype(f16)[None], (PEERS, SPREAD, LANES))
    arrived = lax.all_to_all(spread, OWNERS, split_axis=0, concat_axis=0, tiled=True)
    gram, codebook_sums = pl.pallas_call(
        laid_out,
        out_shape=(jax.ShapeDtypeStruct((LANES, D), f32), jax.ShapeDtypeStruct((K, LANES), f32)),
        in_specs=[VMEM],
        out_specs=(VMEM, VMEM),
        compiler_params=params(16),
        name="laid_out",
    )(arrived.astype(f32))
    return gram, coarse_sums, codebook_sums


def solution(mesh):
    finer = Mesh(mesh.devices.reshape(ZS, ZF, YS, YF, X, 2), DP_SUB)
    return jax.shard_map(
        per_device,
        mesh=finer,
        in_specs=(P(DP_SUB, None), P(), P(), P(DP_SUB), P(DP_SUB, None)),
        out_specs=(P(("x", "c"), None), P(DP, ("x", "c")), P(None, ("x", "c"))),
        check_vma=False,
    )
```

```python
import jax
import jax.numpy as jnp
from jax import lax
from jax.experimental import pallas as pl
from jax.experimental.pallas import tpu as pltpu
from jax.sharding import Mesh
from jax.sharding import PartitionSpec as P

D = 1024
M = 64
K = 256
CENTS = 96
LANES = 128
SUBS = 8
GROUPS = 4
CHUNKS = 2
X = 4
YS = 4
YF = 2
ZF = 2
ZS = 6
NEAR = ("zf",)
FAR = ("yf", "ys")
PARTS = 2
OWNERS = NEAR + FAR
PEERS = ZF * YF * YS
DP = ("zs", "zf", "ys", "yf")
DP_SUB = ("zs", "zf", "ys", "yf", "x", "c")
BOOK0 = D
COARSE0 = D + K
ROWS = D + K + CENTS
GP = D // PEERS
BP = K // PEERS
CP = CENTS // PEERS
C0 = GP + BP
PART = C0 + 16
ONE = PART + BP
SPREAD = C0 + 8
bf16 = jnp.bfloat16
f16 = jnp.float16
f32 = jnp.float32
VMEM = pl.BlockSpec(memory_space=pltpu.VMEM)
SMEM = pl.BlockSpec(memory_space=pltpu.SMEM)
HBM = pl.BlockSpec(memory_space=pltpu.HBM)


def params(mib):
    return pltpu.CompilerParams(vmem_limit_bytes=mib * 2**20)


def dot(a, b):
    return jnp.dot(a, b, preferred_element_type=f32)


def columns(core, x):
    return pl.ds(pl.multiple_of((2 * x + core) * LANES, LANES), LANES)


def book_sums(res, codes):
    rows = res.shape[0]
    low_words = K // GROUPS
    group = lax.shift_right_logical(codes, low_words.bit_length() - 1)
    low = codes - group * low_words
    sub = lax.broadcasted_iota(jnp.int32, (SUBS, LANES), 0)
    lane = lax.broadcasted_iota(jnp.int32, (SUBS, LANES), 1)
    select = (lane // (LANES // SUBS) == sub).astype(f32).astype(bf16)
    group = group.astype(f32).astype(bf16)
    which = lax.dot_general(group, select, (((0,), (0,)), ((), ())), preferred_element_type=f32)
    zeros = jnp.zeros_like(res)
    spread = jnp.concatenate([jnp.where(which == g, res, zeros) for g in range(GROUPS)], axis=1)
    word = lax.broadcasted_iota(jnp.int32, (low_words, rows), 0)
    onehot = [(word == low[m : m + 1, :]).astype(bf16) for m in range(SUBS)]
    sums = dot(jnp.concatenate(onehot, axis=0), spread)
    mine = lax.broadcasted_iota(jnp.int32, (low_words, LANES), 1) // (LANES // SUBS)
    totals = []
    for g in range(GROUPS):
        total = jnp.zeros((low_words, LANES), f32)
        for m in range(SUBS):
            part = sums[m * low_words : (m + 1) * low_words, g * LANES : (g + 1) * LANES]
            total = jnp.where(mine == m, part, total)
        totals.append(total)
    return jnp.concatenate(totals, axis=0)


def half_sums(whose, e, rot, cent, codes, assigned, out, turned, arrive=None, wait=None):
    rows = e.shape[0]
    step = rows // CHUNKS
    for i in range(CHUNKS):
        if arrive is not None:
            arrive(i)
        here = slice(i * step, (i + 1) * step)
        for x in range(X):
            turned[x * LANES : (x + 1) * LANES, here] = e[here, columns(whose, x)].T
    wide = 512
    grams, books, cents = D // PARTS, K // PARTS, CENTS // PARTS
    book0, coarse0 = grams, grams + books
    for n in range(D // wide):
        g = dot(turned[...], e[:, n * wide : (n + 1) * wide])
        for x in range(X):
            for k in range(wide // LANES):
                part, row = divmod((n * (wide // LANES) + k) * LANES, grams)
                out[part, x, row : row + LANES, :] = g[
                    x * LANES : (x + 1) * LANES, k * LANES : (k + 1) * LANES
                ].astype(out.dtype)
    if wait is not None:
        wait()
    label = lax.broadcasted_iota(jnp.int32, (CENTS, rows), 0)
    owner = label // CP
    zf, yf, ys = owner // (YF * YS), owner // YS % YF, owner % YS
    sent = (((label % CP) * ZF + zf) * YS + ys) * YF + yf
    named = assigned[...].reshape(1, rows)
    pick = (label == named).astype(bf16)
    send = (sent == named).astype(bf16)
    lanes_of = [columns(whose, x) for x in range(X)]
    c = jnp.concatenate([cent[:, p] for p in lanes_of], axis=1)
    r = jnp.concatenate([rot[:, p] for p in lanes_of], axis=1)
    base = lax.dot_general(pick, c, (((0,), (0,)), ((), ())), preferred_element_type=f32)
    residual = (dot(e[...], r) - base).astype(bf16)
    coarse = dot(send, residual).astype(out.dtype)
    for x in range(X):
        lanes = slice(x * LANES, (x + 1) * LANES)
        subs = pl.ds(pl.multiple_of((2 * x + whose) * SUBS, SUBS), SUBS)
        total = book_sums(residual[:, lanes], codes[subs, :]).astype(out.dtype)
        for part in range(PARTS):
            out[part, x, book0:coarse0, :] = total[part * books : (part + 1) * books]
            out[part, x, coarse0:, :] = coarse[part * cents : (part + 1) * cents, lanes]


def sibling_sums(
    core_ref, place_ref, e_in, rot_in, cent_in, codes_in, assigned_in,
    out, e, rot, cent, codes, assigned, turned, sems,
):
    step = e.shape[0] // CHUNKS
    first = []
    for i in range(CHUNKS):
        here = slice(i * step, (i + 1) * step)
        first.append(pltpu.make_async_copy(e_in.at[here], e.at[here], sems.at[i]))
    pairs = ((assigned_in, assigned), (cent_in, cent), (codes_in, codes), (rot_in, rot))
    copies = [pltpu.make_async_copy(a, b, sems.at[CHUNKS + i]) for i, (a, b) in enumerate(pairs)]
    for copy in first:
        copy.start()

    def arrive(i):
        first[i].wait()
        if i == 0:
            for copy in copies:
                copy.start()

    def wait():
        for copy in copies:
            copy.wait()

    half_sums(1 - core_ref[0], e, rot, cent, codes, assigned, out, turned, arrive, wait)


def own_sums(core_ref, e, rot, cent, codes, assigned, out, turned):
    half_sums(core_ref[0], e, rot, cent, codes, assigned, out, turned)


def chip_sums(mine, theirs, out):
    for part in range(mine.shape[0]):

        def add(x, carry):
            out[part, x] = (mine[part, x] + theirs[part, x].astype(f32)).astype(bf16)
            return carry

        lax.fori_loop(0, X, add, 0)


def first_sums(arrived, out):
    def summed(a, b):
        return arrived[:, a:b, :].astype(f32).sum(axis=0)

    grams, books = D // PARTS, K // PARTS
    coarse = summed(grams + books, ROWS // PARTS)
    zeros = jnp.zeros((PART - C0 - CP, LANES), f32)
    for q in range(out.shape[0]):
        out[q, :GP, :] = summed(q * GP, (q + 1) * GP).astype(bf16)
        out[q, GP:C0, :] = summed(grams + q * BP, grams + (q + 1) * BP).astype(bf16)
        mine = coarse[q * CP : (q + 1) * CP, :]
        out[q, C0:PART, :] = jnp.concatenate([mine, zeros], axis=0).astype(bf16)


def second_sums(arrived, out):
    total = arrived[...].astype(f32).sum(axis=0)
    high = total.astype(bf16)
    low = total - high.astype(f32)
    coarse = jnp.concatenate([total[C0 : C0 + 8], low[C0 : C0 + 8]], axis=0).astype(bf16)
    book = low[GP:C0].astype(bf16)
    for i in range(out.shape[0]):
        out[i, :C0, :] = high[:C0]
        out[i, C0:PART, :] = coarse
        out[i, PART:ONE, :] = book


def owned_sums(place_ref, arrived, coarse_out, mine, *, vectors):
    total = arrived[...].astype(f32).sum(axis=0)
    coarse = total[C0 : C0 + 8] + total[C0 + 8 : C0 + 16]
    row = lax.broadcasted_iota(jnp.int32, (8, LANES), 0)
    own = jnp.where(row == place_ref[0], coarse, 0.0).sum(axis=0, keepdims=True)
    coarse_out[...] = own * (CENTS / vectors) ** 0.5
    gram = total[:GP] * (1.0 / vectors)
    book = (total[GP:C0] + total[PART:ONE]) * (K / vectors) ** 0.5

    def scaled(v):
        top = jnp.max(jnp.abs(v), keepdims=True)
        power = jnp.ceil(jnp.log2(jnp.maximum(top, 2.0**-100)))
        return v * jnp.exp2(-power), jnp.broadcast_to(power, (8, LANES))

    gram, gram_power = scaled(gram)
    book, book_power = scaled(book)
    mine[:GP, :] = gram
    mine[GP:C0, :] = book
    mine[C0:SPREAD, :] = jnp.where(row == 0, gram_power, book_power)


def laid_out(arrived, gram, book):
    for q in range(PEERS):
        power = jnp.exp2(arrived[q, C0:SPREAD, :])
        j, top = q * GP // LANES, q * GP % LANES
        gram[top : top + GP, j * LANES : (j + 1) * LANES] = arrived[q, :GP, :] * power[0:1]
        book[q * BP : (q + 1) * BP, :] = arrived[q, GP:C0, :] * power[1:2]


def per_device(embeddings, rotation, centroids, assignments, codes):
    rows = embeddings.shape[0]
    vectors = rows * lax.axis_size(DP_SUB)
    core = lax.axis_index("c").reshape(1)
    place = lax.axis_index("zs").reshape(1)
    inputs = (embeddings, rotation, centroids, codes.T, assignments)
    inputs = tuple(pltpu.with_memory_space_constraint(v, pltpu.HBM) for v in inputs)
    shape = (PARTS, X, ROWS // PARTS, LANES)
    turned = pltpu.VMEM((X * LANES, rows), bf16)
    theirs, *held = pl.pallas_call(
        sibling_sums,
        out_shape=[jax.ShapeDtypeStruct(shape, bf16)]
        + [jax.ShapeDtypeStruct(v.shape, v.dtype) for v in inputs],
        in_specs=[SMEM] * 2 + [HBM] * 5,
        out_specs=[VMEM] * 6,
        scratch_shapes=[turned, pltpu.SemaphoreType.DMA((CHUNKS + 4,))],
        compiler_params=params(24),
        name="sibling_sums",
    )(core, place, *inputs)
    arrived = lax.ppermute(theirs, "c", [(0, 1), (1, 0)])
    mine = pl.pallas_call(
        own_sums,
        out_shape=jax.ShapeDtypeStruct(shape, f32),
        in_specs=[SMEM] + [VMEM] * 5,
        out_specs=VMEM,
        scratch_shapes=[turned],
        compiler_params=params(24),
        cost_estimate=pl.CostEstimate(flops=4 * 10**9, bytes_accessed=8 * 10**6, transcendentals=0),
        name="own_sums",
    )(core, *held)
    parts = pl.pallas_call(
        chip_sums,
        out_shape=jax.ShapeDtypeStruct(shape, bf16),
        in_specs=[VMEM] * 2,
        out_specs=VMEM,
        compiler_params=params(16),
        name="chip_sums",
    )(mine, arrived)
    parts = parts.reshape(PARTS * X, ROWS // PARTS, LANES)
    arrived = lax.all_to_all(parts, NEAR + ("x",), split_axis=0, concat_axis=0, tiled=True)
    pieces = pl.pallas_call(
        first_sums,
        out_shape=jax.ShapeDtypeStruct((PEERS // PARTS, PART, LANES), bf16),
        in_specs=[VMEM],
        out_specs=VMEM,
        compiler_params=params(16),
        name="first_sums",
    )(arrived)
    arrived = lax.all_to_all(pieces, FAR, split_axis=0, concat_axis=0, tiled=True)
    pieces = pl.pallas_call(
        second_sums,
        out_shape=jax.ShapeDtypeStruct((ZS, ONE, LANES), bf16),
        in_specs=[VMEM],
        out_specs=VMEM,
        compiler_params=params(16),
        name="second_sums",
    )(arrived)
    arrived = lax.all_to_all(pieces, "zs", split_axis=0, concat_axis=0, tiled=True)
    coarse_sums, mine = pl.pallas_call(
        lambda *refs: owned_sums(*refs, vectors=vectors),
        out_shape=(
            jax.ShapeDtypeStruct((1, LANES), f32),
            jax.ShapeDtypeStruct((SPREAD, LANES), f32),
        ),
        in_specs=[SMEM, VMEM],
        out_specs=(VMEM, VMEM),
        compiler_params=params(16),
        name="owned_sums",
    )(place, arrived)
    spread = jnp.broadcast_to(mine.astype(f16)[None], (PEERS, SPREAD, LANES))
    arrived = lax.all_to_all(spread, OWNERS, split_axis=0, concat_axis=0, tiled=True)
    gram, codebook_sums = pl.pallas_call(
        laid_out,
        out_shape=(jax.ShapeDtypeStruct((LANES, D), f32), jax.ShapeDtypeStruct((K, LANES), f32)),
        in_specs=[VMEM],
        out_specs=(VMEM, VMEM),
        compiler_params=params(16),
        name="laid_out",
    )(arrived.astype(f32))
    return gram, coarse_sums, codebook_sums


def solution(mesh):
    finer = Mesh(mesh.devices.reshape(ZS, ZF, YS, YF, X, 2), DP_SUB)
    return jax.shard_map(
        per_device,
        mesh=finer,
        in_specs=(P(DP_SUB, None), P(), P(), P(DP_SUB), P(DP_SUB, None)),
        out_specs=(P(("x", "c"), None), P(DP, ("x", "c")), P(None, ("x", "c"))),
        check_vma=False,
    )
```

```python
import jax
import jax.numpy as jnp
from jax import lax
from jax.experimental import pallas as pl
from jax.experimental.pallas import tpu as pltpu
from jax.sharding import Mesh
from jax.sharding import PartitionSpec as P

D = 1024
M = 64
K = 256
CENTS = 96
LANES = 128
SUBS = 8
GROUPS = 4
CHUNKS = 1
X = 4
YS = 4
YF = 2
ZF = 2
ZS = 6
NEAR = ("zf",)
FAR = ("yf", "ys")
PARTS = 2
OWNERS = NEAR + FAR
PEERS = ZF * YF * YS
DP = ("zs", "zf", "ys", "yf")
DP_SUB = ("zs", "zf", "ys", "yf", "x", "c")
BOOK0 = D
COARSE0 = D + K
ROWS = D + K + CENTS
GP = D // PEERS
BP = K // PEERS
CP = CENTS // PEERS
C0 = GP + BP
PART = C0 + 16
ONE = PART + BP
SPREAD = C0 + 8
bf16 = jnp.bfloat16
f16 = jnp.float16
f32 = jnp.float32
VMEM = pl.BlockSpec(memory_space=pltpu.VMEM)
SMEM = pl.BlockSpec(memory_space=pltpu.SMEM)
HBM = pl.BlockSpec(memory_space=pltpu.HBM)


def params(mib):
    return pltpu.CompilerParams(vmem_limit_bytes=mib * 2**20)


def dot(a, b):
    return jnp.dot(a, b, preferred_element_type=f32)


def columns(core, x):
    return pl.ds(pl.multiple_of((2 * x + core) * LANES, LANES), LANES)


def book_sums(res, codes):
    rows = res.shape[0]
    low_words = K // GROUPS
    group = lax.shift_right_logical(codes, low_words.bit_length() - 1)
    low = codes - group * low_words
    sub = lax.broadcasted_iota(jnp.int32, (SUBS, LANES), 0)
    lane = lax.broadcasted_iota(jnp.int32, (SUBS, LANES), 1)
    select = (lane // (LANES // SUBS) == sub).astype(f32).astype(bf16)
    group = group.astype(f32).astype(bf16)
    which = lax.dot_general(group, select, (((0,), (0,)), ((), ())), preferred_element_type=f32)
    zeros = jnp.zeros_like(res)
    spread = jnp.concatenate([jnp.where(which == g, res, zeros) for g in range(GROUPS)], axis=1)
    word = lax.broadcasted_iota(jnp.int32, (low_words, rows), 0)
    onehot = [(word == low[m : m + 1, :]).astype(bf16) for m in range(SUBS)]
    sums = dot(jnp.concatenate(onehot, axis=0), spread)
    mine = lax.broadcasted_iota(jnp.int32, (low_words, LANES), 1) // (LANES // SUBS)
    totals = []
    for g in range(GROUPS):
        total = jnp.zeros((low_words, LANES), f32)
        for m in range(SUBS):
            part = sums[m * low_words : (m + 1) * low_words, g * LANES : (g + 1) * LANES]
            total = jnp.where(mine == m, part, total)
        totals.append(total)
    return jnp.concatenate(totals, axis=0)


def half_sums(whose, e, rot, cent, codes, assigned, out, turned, arrive=None, wait=None):
    rows = e.shape[0]
    step = rows // CHUNKS
    for i in range(CHUNKS):
        if arrive is not None:
            arrive(i)
        here = slice(i * step, (i + 1) * step)
        for x in range(X):
            turned[x * LANES : (x + 1) * LANES, here] = e[here, columns(whose, x)].T
    wide = 512
    grams, books, cents = D // PARTS, K // PARTS, CENTS // PARTS
    book0, coarse0 = grams, grams + books
    for n in range(D // wide):
        g = dot(turned[...], e[:, n * wide : (n + 1) * wide])
        for x in range(X):
            for k in range(wide // LANES):
                part, row = divmod((n * (wide // LANES) + k) * LANES, grams)
                out[part, x, row : row + LANES, :] = g[
                    x * LANES : (x + 1) * LANES, k * LANES : (k + 1) * LANES
                ].astype(out.dtype)
    if wait is not None:
        wait()
    label = lax.broadcasted_iota(jnp.int32, (CENTS, rows), 0)
    owner = label // CP
    zf, yf, ys = owner // (YF * YS), owner // YS % YF, owner % YS
    sent = (((label % CP) * ZF + zf) * YS + ys) * YF + yf
    named = assigned[...].reshape(1, rows)
    pick = (label == named).astype(bf16)
    send = (sent == named).astype(bf16)
    lanes_of = [columns(whose, x) for x in range(X)]
    c = jnp.concatenate([cent[:, p] for p in lanes_of], axis=1)
    r = jnp.concatenate([rot[:, p] for p in lanes_of], axis=1)
    base = lax.dot_general(pick, c, (((0,), (0,)), ((), ())), preferred_element_type=f32)
    residual = (dot(e[...], r) - base).astype(bf16)
    coarse = dot(send, residual).astype(out.dtype)
    for x in range(X):
        lanes = slice(x * LANES, (x + 1) * LANES)
        subs = pl.ds(pl.multiple_of((2 * x + whose) * SUBS, SUBS), SUBS)
        total = book_sums(residual[:, lanes], codes[subs, :]).astype(out.dtype)
        for part in range(PARTS):
            out[part, x, book0:coarse0, :] = total[part * books : (part + 1) * books]
            out[part, x, coarse0:, :] = coarse[part * cents : (part + 1) * cents, lanes]


def sibling_sums(
    core_ref, place_ref, e_in, rot_in, cent_in, codes_in, assigned_in,
    out, e, rot, cent, codes, assigned, turned, sems,
):
    pairs = ((e_in, e), (assigned_in, assigned), (cent_in, cent), (codes_in, codes), (rot_in, rot))
    copies = [pltpu.make_async_copy(a, b, sems.at[i]) for i, (a, b) in enumerate(pairs)]
    for copy in copies:
        copy.start()

    def arrive(i):
        copies[0].wait()

    def wait():
        for copy in copies[1:]:
            copy.wait()

    half_sums(1 - core_ref[0], e, rot, cent, codes, assigned, out, turned, arrive, wait)


def own_sums(core_ref, e, rot, cent, codes, assigned, out, turned):
    half_sums(core_ref[0], e, rot, cent, codes, assigned, out, turned)


def chip_sums(mine, theirs, out):
    for part in range(mine.shape[0]):

        def add(x, carry):
            out[part, x] = (mine[part, x] + theirs[part, x].astype(f32)).astype(bf16)
            return carry

        lax.fori_loop(0, X, add, 0)


def first_sums(arrived, out):
    def summed(a, b):
        return arrived[:, a:b, :].astype(f32).sum(axis=0)

    grams, books = D // PARTS, K // PARTS
    coarse = summed(grams + books, ROWS // PARTS)
    zeros = jnp.zeros((PART - C0 - CP, LANES), f32)
    for q in range(out.shape[0]):
        out[q, :GP, :] = summed(q * GP, (q + 1) * GP).astype(bf16)
        out[q, GP:C0, :] = summed(grams + q * BP, grams + (q + 1) * BP).astype(bf16)
        mine = coarse[q * CP : (q + 1) * CP, :]
        out[q, C0:PART, :] = jnp.concatenate([mine, zeros], axis=0).astype(bf16)


def second_sums(arrived, out):
    total = arrived[...].astype(f32).sum(axis=0)
    high = total.astype(bf16)
    low = total - high.astype(f32)
    coarse = jnp.concatenate([total[C0 : C0 + 8], low[C0 : C0 + 8]], axis=0).astype(bf16)
    book = low[GP:C0].astype(bf16)
    for i in range(out.shape[0]):
        out[i, :C0, :] = high[:C0]
        out[i, C0:PART, :] = coarse
        out[i, PART:ONE, :] = book


def owned_sums(place_ref, arrived, coarse_out, mine, *, vectors):
    total = arrived[...].astype(f32).sum(axis=0)
    coarse = total[C0 : C0 + 8] + total[C0 + 8 : C0 + 16]
    row = lax.broadcasted_iota(jnp.int32, (8, LANES), 0)
    own = jnp.where(row == place_ref[0], coarse, 0.0).sum(axis=0, keepdims=True)
    coarse_out[...] = own * (CENTS / vectors) ** 0.5
    gram = total[:GP] * (1.0 / vectors)
    book = (total[GP:C0] + total[PART:ONE]) * (K / vectors) ** 0.5

    def scaled(v):
        top = jnp.max(jnp.abs(v), keepdims=True)
        power = jnp.ceil(jnp.log2(jnp.maximum(top, 2.0**-100)))
        return v * jnp.exp2(-power), jnp.broadcast_to(power, (8, LANES))

    gram, gram_power = scaled(gram)
    book, book_power = scaled(book)
    mine[:GP, :] = gram
    mine[GP:C0, :] = book
    mine[C0:SPREAD, :] = jnp.where(row == 0, gram_power, book_power)


def laid_out(arrived, gram, book):
    for q in range(PEERS):
        power = jnp.exp2(arrived[q, C0:SPREAD, :])
        j, top = q * GP // LANES, q * GP % LANES
        gram[top : top + GP, j * LANES : (j + 1) * LANES] = arrived[q, :GP, :] * power[0:1]
        book[q * BP : (q + 1) * BP, :] = arrived[q, GP:C0, :] * power[1:2]


def per_device(embeddings, rotation, centroids, assignments, codes):
    rows = embeddings.shape[0]
    vectors = rows * lax.axis_size(DP_SUB)
    core = lax.axis_index("c").reshape(1)
    place = lax.axis_index("zs").reshape(1)
    inputs = (embeddings, rotation, centroids, codes.T, assignments)
    inputs = tuple(pltpu.with_memory_space_constraint(v, pltpu.HBM) for v in inputs)
    shape = (PARTS, X, ROWS // PARTS, LANES)
    turned = pltpu.VMEM((X * LANES, rows), bf16)
    theirs, *held = pl.pallas_call(
        sibling_sums,
        out_shape=[jax.ShapeDtypeStruct(shape, bf16)]
        + [jax.ShapeDtypeStruct(v.shape, v.dtype) for v in inputs],
        in_specs=[SMEM] * 2 + [HBM] * 5,
        out_specs=[VMEM] * 6,
        scratch_shapes=[turned, pltpu.SemaphoreType.DMA((12,))],
        compiler_params=params(24),
        name="sibling_sums",
    )(core, place, *inputs)
    arrived = lax.ppermute(theirs, "c", [(0, 1), (1, 0)])
    mine = pl.pallas_call(
        own_sums,
        out_shape=jax.ShapeDtypeStruct(shape, f32),
        in_specs=[SMEM] + [VMEM] * 5,
        out_specs=VMEM,
        scratch_shapes=[turned],
        compiler_params=params(24),
        cost_estimate=pl.CostEstimate(flops=4 * 10**9, bytes_accessed=8 * 10**6, transcendentals=0),
        name="own_sums",
    )(core, *held)
    parts = pl.pallas_call(
        chip_sums,
        out_shape=jax.ShapeDtypeStruct(shape, bf16),
        in_specs=[VMEM] * 2,
        out_specs=VMEM,
        compiler_params=params(16),
        name="chip_sums",
    )(mine, arrived)
    parts = parts.reshape(PARTS * X, ROWS // PARTS, LANES)
    arrived = lax.all_to_all(parts, NEAR + ("x",), split_axis=0, concat_axis=0, tiled=True)
    pieces = pl.pallas_call(
        first_sums,
        out_shape=jax.ShapeDtypeStruct((PEERS // PARTS, PART, LANES), bf16),
        in_specs=[VMEM],
        out_specs=VMEM,
        compiler_params=params(16),
        name="first_sums",
    )(arrived)
    arrived = lax.all_to_all(pieces, FAR, split_axis=0, concat_axis=0, tiled=True)
    pieces = pl.pallas_call(
        second_sums,
        out_shape=jax.ShapeDtypeStruct((ZS, ONE, LANES), bf16),
        in_specs=[VMEM],
        out_specs=VMEM,
        compiler_params=params(16),
        name="second_sums",
    )(arrived)
    arrived = lax.all_to_all(pieces, "zs", split_axis=0, concat_axis=0, tiled=True)
    coarse_sums, mine = pl.pallas_call(
        lambda *refs: owned_sums(*refs, vectors=vectors),
        out_shape=(
            jax.ShapeDtypeStruct((1, LANES), f32),
            jax.ShapeDtypeStruct((SPREAD, LANES), f32),
        ),
        in_specs=[SMEM, VMEM],
        out_specs=(VMEM, VMEM),
        compiler_params=params(16),
        name="owned_sums",
    )(place, arrived)
    spread = jnp.broadcast_to(mine.astype(f16)[None], (PEERS, SPREAD, LANES))
    arrived = lax.all_to_all(spread, OWNERS, split_axis=0, concat_axis=0, tiled=True)
    gram, codebook_sums = pl.pallas_call(
        laid_out,
        out_shape=(jax.ShapeDtypeStruct((LANES, D), f32), jax.ShapeDtypeStruct((K, LANES), f32)),
        in_specs=[VMEM],
        out_specs=(VMEM, VMEM),
        compiler_params=params(16),
        name="laid_out",
    )(arrived.astype(f32))
    return gram, coarse_sums, codebook_sums


def solution(mesh):
    finer = Mesh(mesh.devices.reshape(ZS, ZF, YS, YF, X, 2), DP_SUB)
    return jax.shard_map(
        per_device,
        mesh=finer,
        in_specs=(P(DP_SUB, None), P(), P(), P(DP_SUB), P(DP_SUB, None)),
        out_specs=(P(("x", "c"), None), P(DP, ("x", "c")), P(None, ("x", "c"))),
        check_vma=False,
    )
```
